512 devices in a mesh: tower: 2 (over core), dp: 128 (over x, y_hi, z), mp: 2 (over y_lo).
Axes of the slice: x: 4, y: 4 (y_hi: 2, y_lo: 2; y = y_hi * 2 + y_lo), z: 16, core: 2. Of those that a mesh axis runs over, the one named last changes fastest.
Arguments:
- img_feats: bfloat16 [32768, 1536], P('dp'), may hold values from -6 to 6
- txt_feats: bfloat16 [32768, 1024], P('dp'), may hold values from -6 to 6
- w_img: bfloat16 [1536, 1152], P(None, 'mp'), may hold values from -0.15625 to 0.15625
- w_txt: bfloat16 [1024, 1152], P(None, 'mp'), may hold values from -0.1875 to 0.1875
- logit_scale: float32 [1], replicated, may hold values from 4 to 12
- logit_bias: float32 [1], replicated, may hold values from -4 to -1
Outputs:
- img_grad: float32 [1536, 1152], P(('tower', 'dp'), 'mp')
- txt_grad: float32 [1024, 1152], P(('tower', 'dp'), 'mp')
The draws below stay inside these ranges and needn't reach their ends.
All inputs are finite; a program needn't handle non-finite values.
Results may differ from the reference program's by a relative error of at most 0.0035.
Values may be sent and summed in bfloat16 or wider, within the bound.
A program may use at most 64 MiB of HBM per device.

```python
import math
import jax
import jax.numpy as jnp
from jax import lax

D_IMG = 1536
D_TXT = 1024
EMB = 1152
TOK_DEV = 256
HALF_WIN = 2
TOKENS = 32768
N_DP = 128


def block_scale(stream_key, shape, pieces, low, top_value):
    def one(position, shards_of):
        steps = jax.random.uniform(jax.random.fold_in(jax.random.fold_in(stream_key, 6), position), (shards_of,), jnp.float32, low / len(pieces), top_value / len(pieces))
        return jnp.repeat(jnp.exp(steps), shape[position] // shards_of).reshape((-1,) + (1,) * (len(shape) - position - 1))

    loudness = one(*pieces[0])
    for cut in pieces[1:]:
        loudness = loudness * one(*cut)
    return loudness


def noise(key, dims, width, bound, shards=(), dtype=jnp.bfloat16):
    drawn = width * jax.random.normal(key, dims, jnp.float32)
    if shards:
        drawn = drawn * block_scale(key, dims, shards, -0.22, 0.18)
    return jnp.clip(drawn, -bound, bound).astype(dtype)


def setup_inputs(seed: int = 0) -> dict:
    seeds = jax.random.split(jax.random.key(seed), 7)
    return {
        "img_feats": noise(seeds[0], (TOKENS, D_IMG), 1.0, 6.0, ((0, 128),)),
        "txt_feats": noise(seeds[1], (TOKENS, D_TXT), 1.0, 6.0, ((0, 128),)),
        "w_img": noise(seeds[2], (D_IMG, EMB), D_IMG ** -0.5, 0.15625, ((1, 2),)),
        "w_txt": noise(seeds[3], (D_TXT, EMB), D_TXT ** -0.5, 0.1875, ((1, 2),)),
        "logit_scale": jnp.clip(jax.random.uniform(seeds[4], (1,), jnp.float32, 4.0, 12.0), 4.0, 12.0),
        "logit_bias": jnp.clip(jax.random.uniform(seeds[5], (1,), jnp.float32, -4.0, -1.0), -4.0, -1.0),
    }


epsilon = 1e-06

def normalize(feats, weight):
    projected = jnp.dot(feats, weight, preferred_element_type=jnp.float32)
    radius = jnp.sqrt(lax.optimization_barrier(jnp.sum(projected * projected, axis=1)) + epsilon)
    return (projected / radius[:, None], radius)

def side_grad(own_emb, other_emb, logit_scale, logit_bias):
    own_blocks = own_emb.reshape(N_DP, TOK_DEV, EMB)
    partner = other_emb.reshape(N_DP, TOK_DEV, EMB)
    offsets = jnp.arange(-HALF_WIN, HALF_WIN + 1).astype(jnp.int32)
    columns = jnp.arange((2 * HALF_WIN + 1) * TOK_DEV).astype(jnp.int32)[None, :]
    row_ids = jnp.arange(TOK_DEV).astype(jnp.int32)[:, None]
    positive = columns == row_ids + HALF_WIN * TOK_DEV
    labels = jnp.where(positive, jnp.float32(1.0), jnp.float32(-1.0))
    inv_scale = jnp.float32(1.0 / math.sqrt(TOKENS))

    def span_grad(span):
        window = partner[(span + offsets) % N_DP].reshape(-1, EMB)
        own_rows = own_blocks[span]
        logits = logit_scale[0] * lax.dot_general(own_rows, window, (((1,), (1,)), ((), ())), preferred_element_type=jnp.float32) + logit_bias[0]
        coef = (-labels * jax.nn.sigmoid(-labels * logits) * inv_scale).astype(jnp.bfloat16)
        return logit_scale[0] * jnp.dot(coef, window, preferred_element_type=jnp.float32)
    grads = lax.map(span_grad, jnp.arange(N_DP).astype(jnp.int32))
    return grads.reshape(-1, EMB)

def head_grad(feats, normed, radius, grad_unit):
    inner_dot = lax.optimization_barrier(jnp.sum(normed * grad_unit, axis=1))
    grad_proj = ((grad_unit - normed * inner_dot[:, None]) / radius[:, None]).astype(jnp.bfloat16)
    return lax.dot_general(feats, grad_proj, (((0,), (0,)), ((), ())), preferred_element_type=jnp.float32)

def reference(img_feats, txt_feats, w_img, w_txt, logit_scale, logit_bias):
    img_normed, img_radius = normalize(img_feats, w_img)
    txt_normed, txt_radius = normalize(txt_feats, w_txt)
    img_emb = img_normed.astype(jnp.bfloat16)
    txt_emb = txt_normed.astype(jnp.bfloat16)
    grad_img_emb = side_grad(img_emb, txt_emb, logit_scale, logit_bias)
    grad_txt_emb = side_grad(txt_emb, img_emb, logit_scale, logit_bias)
    img_grad = head_grad(img_feats, img_normed, img_radius, grad_img_emb)
    txt_grad = head_grad(txt_feats, txt_normed, txt_radius, grad_txt_emb)
    return (img_grad, txt_grad)
```

```python
import functools
import math

import jax
import jax.numpy as jnp
import numpy as np
from jax import lax
from jax.experimental import pallas as pl
from jax.experimental.pallas import tpu as pltpu
from jax.sharding import PartitionSpec as P

MESH = pl.DeviceIdType.MESH
HALF_WIN = 2
EPS = 1e-06
NX, NYH, CLS = 4, 2, 4
MSGS = 96
F32 = jnp.float32
BF16 = jnp.bfloat16


def row_order(width, dp, piece, padded):
    zh = dp // (NX * NYH * CLS)
    z_count = zh * CLS
    per_x = NYH * z_count * piece
    rows = 2 * CLS * zh * NYH * 2 * padded
    mat = np.zeros((rows, 4 * per_x), np.float32)
    for xr in range(2):
        for zl in range(CLS):
            for zg in range(zh):
                for yh in range(NYH):
                    for half in range(2):
                        for i in range(piece):
                            out = ((((xr * CLS + zl) * zh + zg) * NYH + yh) * 2 + half) * padded + i
                            col = half * 2 * per_x + xr * per_x + yh * z_count * piece + (zg * CLS + zl) * piece + i
                            mat[out, col] = 1.0
    return mat


def col_to_rows(col):
    n = col.shape[0]
    return jnp.transpose(jnp.broadcast_to(col, (n, 128)))[:8]


def rows_to_col(rows):
    n = rows.shape[1]
    return jnp.transpose(jnp.broadcast_to(rows[:1], (128, n)))[:, :1]


def dot_nt(a, b):
    return lax.dot_general(a, b, (((1,), (1,)), ((), ())), preferred_element_type=F32)


def dot_nn(a, b):
    return jnp.dot(a, b, preferred_element_type=F32)


def body(cfg, scale_ref, bias_ref, img_ref, txt_ref, wi_ref, wt_ref, pi_ref, pt_ref, out_img, out_txt, *scratch):
    (feats, weights, perm, feats_t, fx, normed, own, win, acc, sq_out, sq_in, inner_out, inner_in, ssem, rsem, lsem) = scratch[:16]
    rest = scratch[16:]
    dp, tok, d_img, d_txt, cols, chunks = cfg["dp"], cfg["tok"], cfg["d_img"], cfg["d_txt"], cfg["cols"], cfg["chunks"]
    zh_count = dp // (NX * NYH * CLS)
    z_count = zh_count * CLS
    half = tok // 2
    r_img, r_txt, pad = d_img // (2 * dp), d_txt // (2 * dp), cfg["pad"]
    xrows = CLS * zh_count * NYH * 2 * pad
    crow = xrows // CLS
    lrow = crow // zh_count
    names = ("ps", "pr", "gx", "cf", "cb", "l1", "s1", "l2", "st", "l3")
    buf = [dict(zip(names, rest[len(names) * q : len(names) * (q + 1)])) for q in range(len(chunks))]

    t, d, m = lax.axis_index("tower"), lax.axis_index("dp"), lax.axis_index("mp")
    x = d // (NYH * z_count)
    yh = (d // z_count) % NYH
    z = d % z_count
    zl, zg = z % CLS, z // CLS
    h = (m + yh) % 2

    def at(xx, yy, zz):
        return (xx * NYH + yy) * z_count + zz

    partner = (t, d, 1 - m)
    band_dev = {}
    for k in range(-HALF_WIN, HALF_WIN + 1):
        dk = (d + k + dp) % dp
        band_dev[k] = (1 - t, dk, (h + (dk // z_count) % NYH) % 2)
    x_dev = {j: (t, at((x + j) % NX, yh, z), m) for j in (1, 2, 3)}
    z_dev = {j: (t, at(x, yh, (z + j + z_count) % z_count), m) for j in (1, -1, 2, -2)}
    zg_dev = {j: (t, at(x, yh, ((zg + j) % zh_count) * CLS + zl), m) for j in range(1, zh_count)}
    fin_dev = {(1, 0): (1 - t, d, m), (0, 1): (t, at(x, 1 - yh, z), m), (1, 1): (1 - t, at(x, 1 - yh, z), m)}

    peers = [partner] + list(band_dev.values()) + list(x_dev.values()) + list(z_dev.values()) + list(zg_dev.values())
    peers += [fin_dev[0, 1], fin_dev[1, 1]]
    barrier = pltpu.get_barrier_semaphore()
    for dev in peers:
        pl.semaphore_signal(barrier, inc=1, device_id=dev, device_id_type=MESH)

    ids = {}
    started = []

    def copy(key, src, dst, dev):
        n = ids.setdefault(key, len(ids))
        return pltpu.make_async_remote_copy(
            src_ref=src, dst_ref=dst, send_sem=ssem.at[n], recv_sem=rsem.at[n], device_id=dev, device_id_type=MESH
        )

    def send(key, src, dst, dev):
        c = copy(key, src, dst, dev)
        c.start()
        started.append(c)

    def arrive(key, dst, dev):
        copy(key, dst, dst, dev).wait_recv()

    def loads(which):
        f, w, p, wide = ((img_ref, wi_ref, pi_ref, d_img), (txt_ref, wt_ref, pt_ref, d_txt))[which]
        pk = p.shape[1]
        return [
            pltpu.make_async_copy(f, feats.at[:, pl.ds(0, wide)], lsem.at[0]),
            pltpu.make_async_copy(w, weights.at[:, pl.ds(0, wide)], lsem.at[1]),
            pltpu.make_async_copy(p, perm.at[:, pl.ds(0, pk)], lsem.at[2]),
        ]

    def project(which):
        wide = (d_img, d_txt)[which]
        ls = loads(which)
        for c in ls:
            c.start()
        ls[0].wait()
        ls[1].wait()
        normed[...] = dot_nt(feats[:, :wide], weights[:, :wide])
        ls[2].wait()

    def reorder(which):
        wide = (d_img, d_txt)[which]
        pk = (pi_ref, pt_ref)[which].shape[1]
        for xp in range(2):
            a = xp * pk // 2
            b = wide // 2 + a
            part = dot_nt(perm[:, : pk // 2], feats[:, a : a + pk // 2])
            part = part + dot_nt(perm[:, pk // 2 : pk], feats[:, b : b + pk // 2])
            feats_t[xp * 2 * xrows : (xp + 1) * 2 * xrows, :] = part.astype(BF16)

    for which in range(2):
        pl.when(t == which)(functools.partial(project, which))

    proj = normed[...]
    squares = jnp.sum(proj * proj, axis=1, keepdims=True)
    sq_out[...] = col_to_rows(squares)
    pl.semaphore_wait(barrier, len(peers))
    send("sq", sq_out, sq_in, partner)

    for which in range(2):
        pl.when(t == which)(functools.partial(reorder, which))

    arrive("sq", sq_in, partner)
    inv_radius = 1.0 / jnp.sqrt(squares + rows_to_col(sq_in[...]) + EPS)
    unit = normed[...] * inv_radius
    normed[...] = unit
    own[m] = unit.astype(BF16)

    keep = pl.ds(pl.multiple_of(h * half, half), half)
    give = pl.ds(pl.multiple_of((1 - h) * half, half), half)
    order = (0, 1, -1, 2, -2)
    send("e0", own.at[m, give], own.at[m, give], partner)
    for k in order:
        send(("b", k, 0), own.at[m, keep], win.at[HALF_WIN - k, m], band_dev[k])
    send("e1", own.at[m, keep], own.at[m, keep], partner)
    for j in (1, 3, 2):
        xs = pl.ds(pl.multiple_of(((x + j) % NX) * xrows, xrows), xrows)
        send(("f", j), feats_t.at[xs], fx.at[x], x_dev[j])
    arrive("e0", own.at[1 - m, keep], partner)
    for k in order:
        send(("b", k, 1), own.at[1 - m, keep], win.at[HALF_WIN - k, 1 - m], band_dev[k])
    arrive("e1", own.at[1 - m, give], partner)

    scale, bias = scale_ref[0], bias_ref[0]
    inv_scale = F32(1.0 / math.sqrt(tok * dp))
    inner = jnp.zeros((tok, 1), F32)
    for n, k in enumerate(order):
        slot = HALF_WIN + k
        for part in range(2):
            arrive(("b", -k, part), win.at[slot, part], band_dev[k])
        dots = dot_nt(own[0], win[slot, 0]) + dot_nt(own[1], win[slot, 1])
        logits = scale * dots + bias
        if k == 0:
            rows = lax.broadcasted_iota(jnp.int32, (tok, half), 0)
            columns = lax.broadcasted_iota(jnp.int32, (tok, half), 1) + h * half
            labels = jnp.where(rows == columns, F32(1.0), F32(-1.0))
            coef = -labels * jax.nn.sigmoid(-labels * logits) * inv_scale
        else:
            coef = jax.nn.sigmoid(logits) * inv_scale
        coef = coef.astype(BF16)
        inner = inner + jnp.sum(coef.astype(F32) * dots, axis=1, keepdims=True)
        for c in range(2):
            term = dot_nn(coef, win[slot, c])
            if n:
                acc[c] += term
            else:
                acc[c] = term
    inner = inner * scale
    inner_out[...] = col_to_rows(inner)

    send("inner", inner_out, inner_in, partner)
    for q, (c0, w) in enumerate(chunks):
        b = buf[q]
        b["ps"][...] = (scale * acc[1 - m, :, c0 : c0 + w]).astype(BF16)
        send(("p", q), b["ps"], b["pr"], partner)
    arrive("inner", inner_in, partner)
    total_inner = inner + rows_to_col(inner_in[...])

    low, high = pl.ds(0, half), pl.ds(half, half)
    clow, chigh = pl.ds(0, crow // 2), pl.ds(crow // 2, crow // 2)
    left, right, across = (x + 3) % NX, (x + 1) % NX, (x + 2) % NX

    def stage_g(q):
        c0, w = chunks[q]
        b = buf[q]
        arrive(("p", q), b["pr"], partner)
        grad = scale * acc[m, :, c0 : c0 + w] + b["pr"][...].astype(F32)
        grad = (grad - normed[:, c0 : c0 + w] * total_inner) * inv_radius
        b["gx"][x] = grad.astype(BF16)
        send(("x", q, 1), b["gx"].at[x], b["gx"].at[x], x_dev[1])
        send(("x", q, 3), b["gx"].at[x], b["gx"].at[x], x_dev[3])

    def stage_x(q):
        gx = buf[q]["gx"]
        arrive(("x", q, 1), gx.at[left], x_dev[3])
        send(("y", q, 1), gx.at[left, low], gx.at[left, low], x_dev[1])
        arrive(("x", q, 3), gx.at[right], x_dev[1])
        send(("y", q, 3), gx.at[right, high], gx.at[right, high], x_dev[3])

    def stage_c(q):
        b = buf[q]
        gx, cf, cb = b["gx"], b["cf"], b["cb"]
        mine = pl.ds(pl.multiple_of(x * xrows, xrows), xrows)
        total = dot_nn(feats_t[mine], gx[x])
        if q == 0:
            for j in (1, 3, 2):
                arrive(("f", j), fx.at[(x + 4 - j) % NX], x_dev[4 - j])
        total += dot_nn(fx[left], gx[left])
        total += dot_nn(fx[right], gx[right])
        arrive(("y", q, 1), gx.at[across, low], x_dev[3])
        arrive(("y", q, 3), gx.at[across, high], x_dev[1])
        total += dot_nn(fx[across], gx[across])
        for c in range(CLS):
            piece = total[c * crow : (c + 1) * crow]
            cf[c] = piece
            cb[c] = piece.astype(BF16)
        send(("l1", q, 2), cb.at[(zl + 2) % CLS, clow], b["l1"].at[2, clow], z_dev[2])
        send(("l1", q, -2), cb.at[(zl + 2) % CLS, chigh], b["l1"].at[2, chigh], z_dev[-2])
        send(("l1", q, 1), cb.at[(zl + 1) % CLS], b["l1"].at[0], z_dev[1])
        send(("l1", q, -1), cb.at[(zl + 3) % CLS], b["l1"].at[1], z_dev[-1])

    def stage_1(q):
        b = buf[q]
        arrive(("l1", q, 1), b["l1"].at[0], z_dev[-1])
        arrive(("l1", q, -1), b["l1"].at[1], z_dev[1])
        arrive(("l1", q, 2), b["l1"].at[2, clow], z_dev[-2])
        arrive(("l1", q, -2), b["l1"].at[2, chigh], z_dev[2])
        total = b["cf"][zl] + b["l1"][0].astype(F32) + b["l1"][1].astype(F32) + b["l1"][2].astype(F32)
        for g in range(zh_count):
            b["s1"][g] = total[g * lrow : (g + 1) * lrow]
        for j in range(1, zh_count):
            send(("l2", q, j), b["s1"].at[(zg + j) % zh_count], b["l2"].at[j], zg_dev[j])

    def stage_2(q):
        b = buf[q]
        total = b["s1"][zg]
        for j in range(1, zh_count):
            arrive(("l2", q, j), b["l2"].at[j], zg_dev[zh_count - j])
            total = total + b["l2"][j]
        for p in range(2 * NYH):
            b["st"][p // 2, p % 2, :pad] = total[p * pad : (p + 1) * pad]
        for (dt, dy), dev in fin_dev.items():
            tt, yy = (t + dt) % 2, (yh + dy) % 2
            send(("l3", q, dt, dy), b["st"].at[yy, tt], b["l3"].at[t, dy], dev)
        b["l3"][t, 0] = b["st"][yh, t]

    def stage_3(q):
        c0, w = chunks[q]
        b = buf[q]
        for (dt, dy), dev in fin_dev.items():
            arrive(("l3", q, dt, dy), b["l3"].at[(t + dt) % 2, dy], dev)
        out_img[:, c0 : c0 + w] = (b["l3"][0, 0] + b["l3"][0, 1])[:r_img]
        out_txt[:, c0 : c0 + w] = (b["l3"][1, 0] + b["l3"][1, 1])[:r_txt]

    stages = (stage_g, stage_x, stage_c, stage_1, stage_2, stage_3)
    for step in range(len(stages) + len(chunks) - 1):
        for q in range(len(chunks)):
            if 0 <= step - q < len(stages):
                stages[step - q](q)
    for c in started:
        c.wait_send()


def local(cfg, img_feats, txt_feats, w_img, w_txt, logit_scale, logit_bias):
    dp = lax.axis_size("dp")
    tok, d_img = img_feats.shape
    d_txt = txt_feats.shape[1]
    cols = w_img.shape[1]
    r_img, r_txt = d_img // (2 * dp), d_txt // (2 * dp)
    pad = max(r_img, r_txt)
    chunks = cfg["chunks"](cols)
    cfg = dict(dp=dp, tok=tok, d_img=d_img, d_txt=d_txt, cols=cols, chunks=chunks, pad=pad)
    perm_img = jnp.asarray(row_order(d_img, dp, r_img, pad), BF16)
    perm_txt = jnp.asarray(row_order(d_txt, dp, r_txt, pad), BF16)
    zh_count = dp // (NX * NYH * CLS)
    half = tok // 2
    xrows = CLS * zh_count * NYH * 2 * pad
    crow = xrows // CLS
    lrow = crow // zh_count
    wide = max(d_img, d_txt)
    scratch = [
        pltpu.VMEM((tok, wide), BF16),
        pltpu.VMEM((cols, wide), BF16),
        pltpu.VMEM((2 * xrows, max(perm_img.shape[1], perm_txt.shape[1])), BF16),
        pltpu.VMEM((NX * xrows, tok), BF16),
        pltpu.VMEM((NX, xrows, tok), BF16),
        pltpu.VMEM((tok, cols), F32),
        pltpu.VMEM((2, tok, cols), BF16),
        pltpu.VMEM((2 * HALF_WIN + 1, 2, half, cols), BF16),
        pltpu.VMEM((2, tok, cols), F32),
        pltpu.VMEM((8, tok), F32),
        pltpu.VMEM((8, tok), F32),
        pltpu.VMEM((8, tok), F32),
        pltpu.VMEM((8, tok), F32),
        pltpu.SemaphoreType.DMA((MSGS,)),
        pltpu.SemaphoreType.DMA((MSGS,)),
        pltpu.SemaphoreType.DMA((3,)),
    ]
    for _, w in chunks:
        scratch += [
            pltpu.VMEM((tok, w), BF16),
            pltpu.VMEM((tok, w), BF16),
            pltpu.VMEM((NX, tok, w), BF16),
            pltpu.VMEM((CLS, crow, w), F32),
            pltpu.VMEM((CLS, crow, w), BF16),
            pltpu.VMEM((3, crow, w), BF16),
            pltpu.VMEM((zh_count, lrow, w), F32),
            pltpu.VMEM((zh_count, lrow, w), F32),
            pltpu.VMEM((NYH, 2, 8, w), F32),
            pltpu.VMEM((2, NYH, 8, w), F32),
        ]
    anyspace = pl.BlockSpec(memory_space=pl.ANY)
    smem = pl.BlockSpec(memory_space=pltpu.SMEM)
    vmem = pl.BlockSpec(memory_space=pltpu.VMEM)
    return pl.pallas_call(
        functools.partial(body, cfg),
        out_shape=(jax.ShapeDtypeStruct((r_img, cols), F32), jax.ShapeDtypeStruct((r_txt, cols), F32)),
        in_specs=[smem, smem] + [anyspace] * 6,
        out_specs=(vmem, vmem),
        scratch_shapes=scratch,
        compiler_params=pltpu.CompilerParams(
            collective_id=0, has_side_effects=True, vmem_limit_bytes=44 * 1024 * 1024
        ),
    )(logit_scale, logit_bias, img_feats, txt_feats, w_img.T, w_txt.T, perm_img, perm_txt)


def column_chunks(cols):
    if cols <= 256:
        return ((0, cols),)
    return ((0, 256), (256, cols - 256))


def solution(mesh):
    placed = (P("dp", None), P("dp", None), P(None, "mp"), P(None, "mp"), P(), P())
    return jax.shard_map(
        functools.partial(local, dict(chunks=column_chunks)),
        mesh=mesh,
        in_specs=placed,
        out_specs=(P(("tower", "dp"), "mp"), P(("tower", "dp"), "mp")),
        check_vma=False,
    )
```

```python
import functools
import math

import jax
import jax.numpy as jnp
from jax import lax
from jax.experimental import pallas as pl
from jax.experimental.pallas import tpu as pltpu
from jax.sharding import PartitionSpec as P

MESH = pl.DeviceIdType.MESH
EPS = 1e-06
NX, NYH, CLS = 4, 2, 4
MSGS = 128
F32 = jnp.float32
BF16 = jnp.bfloat16


def dot_nt(a, b):
    return lax.dot_general(a, b, (((1,), (1,)), ((), ())), preferred_element_type=F32)


def dot_nn(a, b):
    return jnp.dot(a, b, preferred_element_type=F32)


def col_to_rows(col):
    n = col.shape[0]
    return jnp.transpose(jnp.broadcast_to(col, (n, 128)))[:8]


def body(cfg, scale_ref, bias_ref, img_ref, txt_ref, wi_ref, wt_ref, out_img, out_txt, *scratch):
    (smem, feats, weights, perm, feats_t, fx, normed, own_t, own_n, win, acc) = scratch[:11]
    (sq_out, sq_in, inner_out, inner_in, ssem, rsem, lsem) = scratch[11:18]
    rest = scratch[18:]
    dp, tok, widths, chunks = cfg["dp"], cfg["tok"], cfg["widths"], cfg["chunks"]
    zgs = dp // (NX * NYH * CLS)
    zs = zgs * CLS
    half = tok // 2
    pieces = [w // (2 * dp) for w in widths]
    names = ("ps", "pr", "gx", "cb", "l1", "xf", "xs", "xr", "st", "l2")
    buf = [dict(zip(names, rest[len(names) * q : len(names) * (q + 1)])) for q in range(len(chunks))]

    t, d, m = lax.axis_index("tower"), lax.axis_index("dp"), lax.axis_index("mp")
    x = d // (NYH * zs)
    yh = (d // zs) % NYH
    z = d % zs
    zl, zg = z % CLS, z // CLS
    h = (m + yh) % 2

    def at(xx, yy, zz):
        return (xx * NYH + yy) * zs + zz

    def along_z(dz, dy):
        return (t, at(x, (yh + dy) % NYH, (z + dz + zs) % zs), m)

    def block(k):
        b = (d + k + dp) % dp
        return b, (h + (b // zs) % NYH) % 2

    partner = (t, d, 1 - m)
    cross = {k: (1 - t,) + block(k) for k in (0, 1, -1)}
    onward = {k: (t,) + block(k) for k in (1, -1)}
    x_dev = {j: (t, at((x + j) % NX, yh, z), m) for j in (1, 2, 3)}
    two = {}
    for dy in range(NYH):
        yy = (yh + dy) % NYH
        two[dy] = (t, at(x, yy, (z + 2 - 4 * yy + zs) % zs), m)
    last = {(j, dt): ((t + dt) % 2, at(x, yh, ((zg + j) % zgs) * CLS + zl), m) for j in range(zgs) for dt in range(2)}
    del last[0, 0]

    peers = [cross[0], cross[1], cross[-1], onward[1], onward[-1]]
    peers += [along_z(dz, dy) for dz in (1, -1, 2, -2) for dy in range(NYH)]
    peers += [dev for (j, dt), dev in last.items() if j]
    peers += list(x_dev.values()) + [along_z(0, 1), partner]
    barrier = pltpu.get_barrier_semaphore()
    for dev in peers:
        pl.semaphore_signal(barrier, inc=1, device_id=dev, device_id_type=MESH)

    ids = {}
    started = {0: [], 1: [], None: []}

    def copy(key, src, dst, dev):
        n = ids.setdefault(key, len(ids))
        return pltpu.make_async_remote_copy(
            src_ref=src, dst_ref=dst, send_sem=ssem.at[n], recv_sem=rsem.at[n], device_id=dev, device_id_type=MESH
        )

    def send(key, src, dst, dev, which=None, like=None):
        copy(key, src, dst, dev).start()
        started[which].append((key, like or (lambda: dst)))

    def arrive(key, dst):
        copy(key, dst, dst, partner).wait_recv()

    def by_tower(fn, *args):
        for which in range(2):
            pl.when(t == which)(functools.partial(fn, which, *args))

    def project(which):
        f, w, wide = (img_ref, txt_ref)[which], (wi_ref, wt_ref)[which], widths[which]
        loads = [
            pltpu.make_async_copy(f, feats.at[:, pl.ds(0, wide)], lsem.at[0]),
            pltpu.make_async_copy(w, weights.at[:, pl.ds(0, wide)], lsem.at[1]),
            pltpu.make_async_copy(scale_ref, smem.at[0], lsem.at[2]),
            pltpu.make_async_copy(bias_ref, smem.at[1], lsem.at[3]),
        ]
        for c in loads:
            c.start()
        for c in loads:
            c.wait()
        normed[...] = dot_nt(weights[:, :wide], feats[:, :wide])

    def reorder(which):
        wide, r = widths[which], pieces[which]
        n = wide // 2
        row = lax.broadcasted_iota(jnp.int32, (n, 128), 0)
        p = (row * ((65536 + r - 1) // r)) >> 16
        i = row - p * r
        zbits = zgs.bit_length() - 1
        hf, g, y, c, xr = p & 1, (p >> 1) & (zgs - 1), (p >> (1 + zbits)) & 1, (p >> (2 + zbits)) & 3, p >> (4 + zbits)
        col = ((hf * 2 + xr) * NYH + y) * (zs * r) + (g * CLS + c) * r + i
        lane = lax.broadcasted_iota(jnp.int32, (n, 128), 1)
        for c0 in range(0, n, 128):
            cw = min(128, n - c0)
            perm[:n, c0 : c0 + cw] = jnp.where(col == lane + c0, F32(1.0), F32(0.0)).astype(BF16)[:, :cw]
        for xp in range(2):
            a = xp * n // 2
            part = dot_nt(perm[:n, : n // 2], feats[:, a : a + n // 2])
            part = part + dot_nt(perm[:n, n // 2 : n], feats[:, n + a : n + a + n // 2])
            feats_t[xp * n : (xp + 1) * n, :] = part.astype(BF16)
        rows = wide // NX
        for j in (1, 3, 2):
            xs = pl.ds(pl.multiple_of(((x + j) % NX) * rows, 16), rows)
            send(("f", j), feats_t.at[xs], fx.at[x, pl.ds(0, rows)], x_dev[j], which, lambda: fx.at[0, pl.ds(0, rows)])

    by_tower(project)
    squares = jnp.sum(normed[...] * normed[...], axis=0, keepdims=True)
    sq_out[...] = jnp.broadcast_to(squares, sq_out.shape)
    pl.semaphore_wait(barrier, len(peers))
    send("sq", sq_out, sq_in, partner)
    arrive("sq", sq_in)
    inv_radius = 1.0 / jnp.sqrt(squares + sq_in[:1] + EPS)
    unit = normed[...] * inv_radius
    normed[...] = unit
    unit = unit.astype(BF16)
    for th in range(2):
        own_t[m, th] = unit[:, th * half : (th + 1) * half]

    send("e0", own_t.at[m, 1 - h], own_t.at[m, 1 - h], partner)
    for s in (1, -1, 0):
        send(("b", s, 0), own_t.at[m, h], win.at[2 - s, m], cross[s])
    send("e1", own_t.at[m, h], own_t.at[m, h], partner)
    by_tower(reorder)
    arrive("e0", own_t.at[1 - m, h])
    for s in (1, -1, 0):
        send(("b", s, 1), own_t.at[1 - m, h], win.at[2 - s, 1 - m], cross[s])
    for f in range(2):
        for s in (1, -1):
            side = cross[-s][2]
            c = side if f == 0 else 1 - side
            arrive(("b", s, f), win.at[2 - s, c])
            send(("w", s, f), win.at[2 - s, c], win.at[2 - 2 * s, c], onward[s])
        if f == 0:
            arrive("e1", own_t.at[1 - m, 1 - h])
            for c in range(2):
                for th in range(2):
                    own_n[c, th * half : (th + 1) * half, :] = jnp.transpose(own_t[c, th])

    scale, bias = smem[0, 0], smem[1, 0]
    inv_scale = F32(1.0 / math.sqrt(tok * dp))
    inner = jnp.zeros((tok, half), F32)
    for n, k in enumerate((0, 1, -1, 2, -2)):
        slot = 2 + k
        if k == 0:
            for f in range(2):
                arrive(("b", 0, f), win.at[slot, f])
        if abs(k) == 2:
            for f in range(2):
                arrive(("w", -k // 2, f), win.at[slot, f])
        dots = dot_nn(own_n[0], win[slot, 0]) + dot_nn(own_n[1], win[slot, 1])
        logits = scale * dots + bias
        if k == 0:
            rows = lax.broadcasted_iota(jnp.int32, (tok, half), 0)
            columns = lax.broadcasted_iota(jnp.int32, (tok, half), 1) + h * half
            labels = jnp.where(rows == columns, F32(1.0), F32(-1.0))
            coef = -labels * jax.nn.sigmoid(-labels * logits) * inv_scale
        else:
            coef = jax.nn.sigmoid(logits) * inv_scale
        coef = coef.astype(BF16)
        inner = inner + coef.astype(F32) * dots
        for c in range(2):
            term = dot_nt(win[slot, c], coef)
            if n:
                acc[c] += term
            else:
                acc[c] = term
    inner_out[...] = scale * col_to_rows(jnp.sum(inner, axis=1, keepdims=True))
    send("inner", inner_out, inner_in, partner)
    for q, (c0, w, _) in enumerate(chunks):
        b = buf[q]
        b["ps"][...] = (scale * acc[1 - m, c0 : c0 + w]).astype(BF16)
        send(("p", q), b["ps"], b["pr"], partner)
    arrive("inner", inner_in)
    total_inner = inner_out[:1] + inner_in[:1]

    def stage_g(q):
        c0, w, z_first = chunks[q]
        b = buf[q]
        arrive(("p", q), b["pr"])
        grad = scale * acc[m, c0 : c0 + w] + b["pr"][...].astype(F32)
        grad = (grad - normed[c0 : c0 + w] * total_inner) * inv_radius
        own = 0 if z_first else x
        b["gx"][own] = grad.astype(BF16)
        if z_first:
            by_tower(part_products, q)
        else:
            for j in (2, 1, 3):
                send(("x", q, j), b["gx"].at[x], b["gx"].at[x], x_dev[j])

    def send_classes(which, q, br):
        cb, l1 = buf[q]["cb"], buf[q]["l1"]
        rows = pl.ds(0, br)

        def go(slot, c, dy, dev):
            send(("l1", q, slot), cb.at[c % CLS, (yh + dy) % NYH, :, rows], l1.at[slot, :, rows], dev, which, lambda: l1.at[0, :, pl.ds(0, br)])

        for dy in (1, 0):
            go(4 + dy, zl + 2, dy, two[dy])
        for dy in (1, 0):
            go(0 + dy, zl + 1, dy, along_z(1, dy))
            go(2 + dy, zl + 3, dy, along_z(-1, dy))
        go(6, zl, 1, along_z(0, 1))

    def part_products(which, q):
        b = buf[q]
        rows = widths[which] // NX
        br = rows // (CLS * NYH)
        for xx in range(NX):
            total = dot_nt(feats_t[xx * rows : (xx + 1) * rows], b["gx"][0]).astype(BF16)
            for c in range(CLS):
                for y in range(NYH):
                    o = (c * NYH + y) * br
                    b["cb"][c, y, xx, :br] = total[o : o + br]
        send_classes(which, q, br)

    def x_products(which, q):
        b = buf[q]
        gx = b["gx"]
        rows = widths[which] // NX
        br = rows // (CLS * NYH)
        mine = pl.ds(pl.multiple_of(x * rows, 16), rows)
        total = dot_nt(feats_t[mine], gx[x])
        for j in (1, 3, 2):
            src = (x + NX - j) % NX
            if q == first_x:
                arrive(("f", j), fx.at[src, pl.ds(0, rows)])
            arrive(("x", q, j), gx.at[src])
            total += dot_nt(fx[src, :rows], gx[src])
        total = total.astype(BF16)
        for c in range(CLS):
            for y in range(NYH):
                o = (c * NYH + y) * br
                b["cb"][c, y, 0, :br] = total[o : o + br]
        send_classes(which, q, br)

    def class_sum(which, q):
        b = buf[q]
        z_first = chunks[q][2]
        r = pieces[which]
        br = widths[which] // (NX * CLS * NYH)
        for slot in range(7):
            arrive(("l1", q, slot), b["l1"].at[slot, :, pl.ds(0, br)])

        def total(xx):
            s = b["cb"][zl, yh, xx, :br].astype(F32)
            for slot in range(7):
                s = s + b["l1"][slot, xx, :br].astype(F32)
            return s

        if z_first:
            for xx in range(NX):
                s = total(xx)
                b["xf"][xx, :br] = s
                b["xs"][xx, :br] = s.astype(BF16)
            for j in (2, 1, 3):
                src = b["xs"].at[(x + j) % NX, pl.ds(0, br)]
                like = lambda: b["xr"].at[0, pl.ds(0, br)]
                send(("xr", q, j), src, b["xr"].at[j, pl.ds(0, br)], x_dev[j], which, like)
        else:
            send_last(which, q, total(0))

    def x_sum(which, q):
        b = buf[q]
        br = widths[which] // (NX * CLS * NYH)
        s = b["xf"][x, :br]
        for j in (1, 3, 2):
            arrive(("xr", q, j), b["xr"].at[j, pl.ds(0, br)])
            s = s + b["xr"][j, :br].astype(F32)
        send_last(which, q, s)

    def send_last(which, q, s):
        st, l2 = buf[q]["st"], buf[q]["l2"]
        r = pieces[which]
        for g in range(zgs):
            for hf in range(2):
                o = (g * 2 + hf) * r
                st[g, hf, :r] = s[o : o + r]
        l2[t, 0] = st[zg, t]
        for (j, dt), dev in last.items():
            send(("l2", q, j, dt), st.at[(zg + j) % zgs, (t + dt) % 2], l2.at[t, j], dev, which, lambda: l2.at[0, 0])

    def finish(q):
        c0, w, _ = chunks[q]
        l2 = buf[q]["l2"]
        for j, dt in last:
            arrive(("l2", q, j, dt), l2.at[(t + dt) % 2, j])
        a, b = l2[0, 0], l2[1, 0]
        for j in range(1, zgs):
            a, b = a + l2[0, j], b + l2[1, j]
        out_img[:, c0 : c0 + w] = a[: pieces[0]]
        out_txt[:, c0 : c0 + w] = b[: pieces[1]]

    first_x = min(q for q, c in enumerate(chunks) if not c[2])
    for stage, q in cfg["order"](chunks):
        if stage == "g":
            stage_g(q)
        elif stage == "c":
            by_tower(x_products, q)
        elif stage == "1":
            by_tower(class_sum, q)
        elif stage == "x":
            by_tower(x_sum, q)
        else:
            finish(q)

    def drain(which):
        for key, like in started[which]:
            copy(key, like(), like(), partner).wait_send()

    by_tower(drain)
    drain(None)


def local(cfg, img_feats, txt_feats, w_img, w_txt, logit_scale, logit_bias):
    dp = lax.axis_size("dp")
    tok = img_feats.shape[0]
    widths = (img_feats.shape[1], txt_feats.shape[1])
    cols = w_img.shape[1]
    chunks = cfg["chunks"](cols)
    cfg = dict(cfg, dp=dp, tok=tok, widths=widths, chunks=chunks)
    zgs = dp // (NX * NYH * CLS)
    half = tok // 2
    wide = max(widths)
    rows = wide // NX
    br = rows // (CLS * NYH)
    pieces = [w // (2 * dp) for w in widths]
    scratch = [
        pltpu.SMEM((2, 1), F32),
        pltpu.VMEM((tok, wide), BF16),
        pltpu.VMEM((cols, wide), BF16),
        pltpu.VMEM((wide // 2, wide // 2), BF16),
        pltpu.VMEM((wide, tok), BF16),
        pltpu.VMEM((NX, rows, tok), BF16),
        pltpu.VMEM((cols, tok), F32),
        pltpu.VMEM((2, 2, cols, half), BF16),
        pltpu.VMEM((2, tok, cols), BF16),
        pltpu.VMEM((5, 2, cols, half), BF16),
        pltpu.VMEM((2, cols, tok), F32),
        pltpu.VMEM((8, tok), F32),
        pltpu.VMEM((8, tok), F32),
        pltpu.VMEM((8, tok), F32),
        pltpu.VMEM((8, tok), F32),
        pltpu.SemaphoreType.DMA((MSGS,)),
        pltpu.SemaphoreType.DMA((MSGS,)),
        pltpu.SemaphoreType.DMA((4,)),
    ]
    for _, w, z_first in chunks:
        xb = NX if z_first else 1
        xz = br if z_first else 16
        scratch += [
            pltpu.VMEM((w, tok), BF16),
            pltpu.VMEM((w, tok), BF16),
            pltpu.VMEM((1 if z_first else NX, w, tok), BF16),
            pltpu.VMEM((CLS, NYH, xb, br, w), BF16),
            pltpu.VMEM((7, xb, br, w), BF16),
            pltpu.VMEM((NX, xz, w), F32),
            pltpu.VMEM((NX, xz, w), BF16),
            pltpu.VMEM((NX, xz, w), BF16),
            pltpu.VMEM((zgs, 2, 8, w), F32),
            pltpu.VMEM((2, zgs, 8, w), F32),
        ]
    hbm = pl.BlockSpec(memory_space=pltpu.HBM)
    vmem = pl.BlockSpec(memory_space=pltpu.VMEM)
    return pl.pallas_call(
        functools.partial(body, cfg),
        out_shape=tuple(jax.ShapeDtypeStruct((r, cols), F32) for r in pieces),
        in_specs=[hbm] * 6,
        out_specs=(vmem, vmem),
        scratch_shapes=scratch,
        compiler_params=pltpu.CompilerParams(
            collective_id=0, has_side_effects=True, vmem_limit_bytes=61 * 1024 * 1024
        ),
    )(logit_scale, logit_bias, img_feats, txt_feats, w_img.T, w_txt.T)


def column_chunks(cols):
    return ((0, 256, False), (256, cols - 256, False))


def stage_order(chunks):
    steps = ["gc1l", "g1xl"]
    out = []
    for step in range(4 + len(chunks)):
        for q, c in enumerate(chunks):
            if 0 <= step - q < 4:
                out.append((steps[c[2]][step - q], q))
    return out


def solution(mesh):
    placed = (P("dp", None), P("dp", None), P(None, "mp"), P(None, "mp"), P(), P())
    return jax.shard_map(
        functools.partial(local, dict(chunks=column_chunks, order=stage_order)),
        mesh=mesh,
        in_specs=placed,
        out_specs=(P(("tower", "dp"), "mp"), P(("tower", "dp"), "mp")),
        check_vma=False,
    )
```

```python
import functools
import math

import jax
import jax.numpy as jnp
from jax import lax
from jax.experimental import pallas as pl
from jax.experimental.pallas import tpu as pltpu
from jax.sharding import PartitionSpec as P

MESH = pl.DeviceIdType.MESH
EPS = 1e-06
NX, NYH, CLS = 4, 2, 4
MSGS = 128
F32 = jnp.float32
BF16 = jnp.bfloat16


def dot_nt(a, b):
    return lax.dot_general(a, b, (((1,), (1,)), ((), ())), preferred_element_type=F32)


def dot_nn(a, b):
    return jnp.dot(a, b, preferred_element_type=F32)


def col_to_rows(col):
    n = col.shape[0]
    return jnp.transpose(jnp.broadcast_to(col, (n, 128)))[:8]


def body(cfg, scale_ref, bias_ref, img_ref, txt_ref, wi_ref, wt_ref, out_img, out_txt, *scratch):
    (smem, feats, weights, perm, feats_t, fx, normed, own_t, own_n, win, acc) = scratch[:11]
    (sq_out, sq_in, inner_out, inner_in, ssem, rsem, lsem) = scratch[11:18]
    rest = scratch[18:]
    dp, tok, widths, chunks = cfg["dp"], cfg["tok"], cfg["widths"], cfg["chunks"]
    zgs = dp // (NX * NYH * CLS)
    zs = zgs * CLS
    half = tok // 2
    pieces = [w // (2 * dp) for w in widths]
    names = ("ps", "pr", "gx", "cb", "l1", "xf", "xs", "xr", "st", "l2")
    buf = [dict(zip(names, rest[len(names) * q : len(names) * (q + 1)])) for q in range(len(chunks))]

    t, d, m = lax.axis_index("tower"), lax.axis_index("dp"), lax.axis_index("mp")
    x = d // (NYH * zs)
    yh = (d // zs) % NYH
    z = d % zs
    zl, zg = z % CLS, z // CLS
    h = (m + yh) % 2

    def at(xx, yy, zz):
        return (xx * NYH + yy) * zs + zz

    def along_z(dz, dy):
        return (t, at(x, (yh + dy) % NYH, (z + dz + zs) % zs), m)

    def block(k):
        b = (d + k + dp) % dp
        return b, (h + (b // zs) % NYH) % 2

    partner = (t, d, 1 - m)
    cross = {k: (1 - t,) + block(k) for k in (0, 1, -1)}
    onward = {k: (t,) + block(k) for k in (1, -1)}
    x_dev = {j: (t, at((x + j) % NX, yh, z), m) for j in (1, 2, 3)}
    two = {}
    for dy in range(NYH):
        yy = (yh + dy) % NYH
        two[dy] = (t, at(x, yy, (z + 2 - 4 * yy + zs) % zs), m)
    last = {(j, dt): ((t + dt) % 2, at(x, yh, ((zg + j) % zgs) * CLS + zl), m) for j in range(zgs) for dt in range(2)}
    del last[0, 0]

    peers = [cross[0], cross[1], cross[-1], onward[1], onward[-1]]
    peers += [along_z(dz, dy) for dz in (1, -1, 2, -2) for dy in range(NYH)]
    peers += [dev for (j, dt), dev in last.items() if j]
    peers += list(x_dev.values()) + [along_z(0, 1), partner]
    barrier = pltpu.get_barrier_semaphore()
    for dev in peers:
        pl.semaphore_signal(barrier, inc=1, device_id=dev, device_id_type=MESH)

    ids = {}
    started = {0: [], 1: [], None: []}

    def copy(key, src, dst, dev):
        n = ids.setdefault(key, len(ids))
        return pltpu.make_async_remote_copy(
            src_ref=src, dst_ref=dst, send_sem=ssem.at[n], recv_sem=rsem.at[n], device_id=dev, device_id_type=MESH
        )

    def send(key, src, dst, dev, which=None, like=None):
        copy(key, src, dst, dev).start()
        started[which].append((key, like or (lambda: dst)))

    def arrive(key, dst):
        copy(key, dst, dst, partner).wait_recv()

    def by_tower(fn, *args):
        for which in range(2):
            pl.when(t == which)(functools.partial(fn, which, *args))

    def project(which):
        f, w, wide = (img_ref, txt_ref)[which], (wi_ref, wt_ref)[which], widths[which]
        loads = [
            pltpu.make_async_copy(f, feats.at[:, pl.ds(0, wide)], lsem.at[0]),
            pltpu.make_async_copy(w, weights.at[:, pl.ds(0, wide)], lsem.at[1]),
            pltpu.make_async_copy(scale_ref, smem.at[0], lsem.at[2]),
            pltpu.make_async_copy(bias_ref, smem.at[1], lsem.at[3]),
        ]
        for c in loads:
            c.start()
        for c in loads:
            c.wait()
        normed[...] = dot_nt(weights[:, :wide], feats[:, :wide])

    def reorder(which):
        wide, r = widths[which], pieces[which]
        n = wide // 2
        row = lax.broadcasted_iota(jnp.int32, (n, 128), 0)
        p = (row * ((65536 + r - 1) // r)) >> 16
        i = row - p * r
        zbits = zgs.bit_length() - 1
        hf, g, y, c, xr = p & 1, (p >> 1) & (zgs - 1), (p >> (1 + zbits)) & 1, (p >> (2 + zbits)) & 3, p >> (4 + zbits)
        col = ((hf * 2 + xr) * NYH + y) * (zs * r) + (g * CLS + c) * r + i
        lane = lax.broadcasted_iota(jnp.int32, (n, 128), 1)
        for c0 in range(0, n, 128):
            cw = min(128, n - c0)
            perm[:n, c0 : c0 + cw] = jnp.where(col == lane + c0, F32(1.0), F32(0.0)).astype(BF16)[:, :cw]
        for xp in range(2):
            a = xp * n // 2
            part = dot_nt(perm[:n, : n // 2], feats[:, a : a + n // 2])
            part = part + dot_nt(perm[:n, n // 2 : n], feats[:, n + a : n + a + n // 2])
            feats_t[xp * n : (xp + 1) * n, :] = part.astype(BF16)
        rows = wide // NX
        for j in (1, 3, 2):
            xs = pl.ds(pl.multiple_of(((x + j) % NX) * rows, 16), rows)
            send(("f", j), feats_t.at[xs], fx.at[x, pl.ds(0, rows)], x_dev[j], which, lambda: fx.at[0, pl.ds(0, rows)])

    by_tower(project)
    squares = jnp.sum(normed[...] * normed[...], axis=0, keepdims=True)
    sq_out[...] = jnp.broadcast_to(squares, sq_out.shape)
    pl.semaphore_wait(barrier, len(peers))
    send("sq", sq_out, sq_in, partner)
    arrive("sq", sq_in)
    inv_radius = 1.0 / jnp.sqrt(squares + sq_in[:1] + EPS)
    unit = normed[...] * inv_radius
    normed[...] = unit
    unit = unit.astype(BF16)
    for th in range(2):
        own_t[m, th] = unit[:, th * half : (th + 1) * half]

    send("e0", own_t.at[m, 1 - h], own_t.at[m, 1 - h], partner)
    for s in (1, -1, 0):
        send(("b", s, 0), own_t.at[m, h], win.at[2 - s, m], cross[s])
    send("e1", own_t.at[m, h], own_t.at[m, h], partner)
    by_tower(reorder)
    arrive("e0", own_t.at[1 - m, h])
    for s in (1, -1, 0):
        send(("b", s, 1), own_t.at[1 - m, h], win.at[2 - s, 1 - m], cross[s])
    for f in range(2):
        for s in (1, -1):
            side = cross[-s][2]
            c = side if f == 0 else 1 - side
            arrive(("b", s, f), win.at[2 - s, c])
            send(("w", s, f), win.at[2 - s, c], win.at[2 - 2 * s, c], onward[s])
        if f == 0:
            arrive("e1", own_t.at[1 - m, 1 - h])
            for c in range(2):
                for th in range(2):
                    own_n[c, th * half : (th + 1) * half, :] = jnp.transpose(own_t[c, th])

    scale, bias = smem[0, 0], smem[1, 0]
    inv_scale = F32(1.0 / math.sqrt(tok * dp))
    inner = jnp.zeros((tok, half), F32)
    for n, k in enumerate((0, 1, -1, 2, -2)):
        slot = 2 + k
        if k == 0:
            for f in range(2):
                arrive(("b", 0, f), win.at[slot, f])
        if abs(k) == 2:
            for f in range(2):
                arrive(("w", -k // 2, f), win.at[slot, f])
        dots = dot_nn(own_n[0], win[slot, 0]) + dot_nn(own_n[1], win[slot, 1])
        logits = scale * dots + bias
        if k == 0:
            rows = lax.broadcasted_iota(jnp.int32, (tok, half), 0)
            columns = lax.broadcasted_iota(jnp.int32, (tok, half), 1) + h * half
            labels = jnp.where(rows == columns, F32(1.0), F32(-1.0))
            coef = -labels * jax.nn.sigmoid(-labels * logits) * inv_scale
        else:
            coef = jax.nn.sigmoid(logits) * inv_scale
        coef = coef.astype(BF16)
        inner = inner + coef.astype(F32) * dots
        for c in range(2):
            term = dot_nt(win[slot, c], coef)
            if n:
                acc[c] += term
            else:
                acc[c] = term
    inner_out[...] = scale * col_to_rows(jnp.sum(inner, axis=1, keepdims=True))
    send("inner", inner_out, inner_in, partner)
    for q, (c0, w, _) in enumerate(chunks):
        b = buf[q]
        b["ps"][...] = (scale * acc[1 - m, c0 : c0 + w]).astype(BF16)
        send(("p", q), b["ps"], b["pr"], partner)
    arrive("inner", inner_in)
    total_inner = inner_out[:1] + inner_in[:1]

    def stage_g(q):
        c0, w, z_first = chunks[q]
        b = buf[q]
        arrive(("p", q), b["pr"])
        grad = scale * acc[m, c0 : c0 + w] + b["pr"][...].astype(F32)
        grad = (grad - normed[c0 : c0 + w] * total_inner) * inv_radius
        own = 0 if z_first else x
        b["gx"][own] = grad.astype(BF16)
        if z_first:
            by_tower(part_products, q)
        else:
            for j in (2, 1, 3):
                send(("x", q, j), b["gx"].at[x], b["gx"].at[x], x_dev[j])

    def send_classes(which, q, br):
        cb, l1 = buf[q]["cb"], buf[q]["l1"]
        rows = pl.ds(0, br)

        def go(slot, c, dy, dev):
            send(("l1", q, slot), cb.at[c % CLS, (yh + dy) % NYH, :, rows], l1.at[slot, :, rows], dev, which, lambda: l1.at[0, :, pl.ds(0, br)])

        for dy in (1, 0):
            go(4 + dy, zl + 2, dy, two[dy])
        for dy in (1, 0):
            go(0 + dy, zl + 1, dy, along_z(1, dy))
            go(2 + dy, zl + 3, dy, along_z(-1, dy))
        go(6, zl, 1, along_z(0, 1))

    def part_products(which, q):
        b = buf[q]
        rows = widths[which] // NX
        br = rows // (CLS * NYH)
        for xx in range(NX):
            total = dot_nt(feats_t[xx * rows : (xx + 1) * rows], b["gx"][0]).astype(BF16)
            for c in range(CLS):
                for y in range(NYH):
                    o = (c * NYH + y) * br
                    b["cb"][c, y, xx, :br] = total[o : o + br]
        send_classes(which, q, br)

    def x_products(which, q):
        b = buf[q]
        gx = b["gx"]
        rows = widths[which] // NX
        br = rows // (CLS * NYH)
        mine = pl.ds(pl.multiple_of(x * rows, 16), rows)
        total = dot_nt(feats_t[mine], gx[x])
        for j in (1, 3, 2):
            src = (x + NX - j) % NX
            if q == first_x:
                arrive(("f", j), fx.at[src, pl.ds(0, rows)])
            arrive(("x", q, j), gx.at[src])
            total += dot_nt(fx[src, :rows], gx[src])
        total = total.astype(BF16)
        for c in range(CLS):
            for y in range(NYH):
                o = (c * NYH + y) * br
                b["cb"][c, y, 0, :br] = total[o : o + br]
        send_classes(which, q, br)

    def class_sum(which, q):
        b = buf[q]
        z_first = chunks[q][2]
        r = pieces[which]
        br = widths[which] // (NX * CLS * NYH)
        for slot in range(7):
            arrive(("l1", q, slot), b["l1"].at[slot, :, pl.ds(0, br)])

        def total(xx):
            s = b["cb"][zl, yh, xx, :br].astype(F32)
            for slot in range(7):
                s = s + b["l1"][slot, xx, :br].astype(F32)
            return s

        if z_first:
            for xx in range(NX):
                s = total(xx)
                b["xf"][xx, :br] = s
                b["xs"][xx, :br] = s.astype(BF16)
            for j in (2, 1, 3):
                src = b["xs"].at[(x + j) % NX, pl.ds(0, br)]
                like = lambda: b["xr"].at[0, pl.ds(0, br)]
                send(("xr", q, j), src, b["xr"].at[j, pl.ds(0, br)], x_dev[j], which, like)
        else:
            send_last(which, q, total(0))

    def x_sum(which, q):
        b = buf[q]
        br = widths[which] // (NX * CLS * NYH)
        s = b["xf"][x, :br]
        for j in (1, 3, 2):
            arrive(("xr", q, j), b["xr"].at[j, pl.ds(0, br)])
            s = s + b["xr"][j, :br].astype(F32)
        send_last(which, q, s)

    def send_last(which, q, s):
        st, l2 = buf[q]["st"], buf[q]["l2"]
        r = pieces[which]
        for g in range(zgs):
            for hf in range(2):
                o = (g * 2 + hf) * r
                st[g, hf, :r] = s[o : o + r]
        l2[t, 0] = st[zg, t]
        for (j, dt), dev in last.items():
            send(("l2", q, j, dt), st.at[(zg + j) % zgs, (t + dt) % 2], l2.at[t, j], dev, which, lambda: l2.at[0, 0])

    def finish(q):
        c0, w, _ = chunks[q]
        l2 = buf[q]["l2"]
        for j, dt in last:
            arrive(("l2", q, j, dt), l2.at[(t + dt) % 2, j])
        a, b = l2[0, 0], l2[1, 0]
        for j in range(1, zgs):
            a, b = a + l2[0, j], b + l2[1, j]
        out_img[:, c0 : c0 + w] = a[: pieces[0]]
        out_txt[:, c0 : c0 + w] = b[: pieces[1]]

    first_x = min(q for q, c in enumerate(chunks) if not c[2])
    for stage, q in cfg["order"](chunks):
        if stage == "g":
            stage_g(q)
        elif stage == "c":
            by_tower(x_products, q)
        elif stage == "1":
            by_tower(class_sum, q)
        elif stage == "x":
            by_tower(x_sum, q)
        else:
            finish(q)

    def drain(which):
        for key, like in started[which]:
            copy(key, like(), like(), partner).wait_send()

    by_tower(drain)
    drain(None)


def local(cfg, img_feats, txt_feats, w_img, w_txt, logit_scale, logit_bias):
    dp = lax.axis_size("dp")
    tok = img_feats.shape[0]
    widths = (img_feats.shape[1], txt_feats.shape[1])
    cols = w_img.shape[1]
    chunks = cfg["chunks"](cols)
    cfg = dict(cfg, dp=dp, tok=tok, widths=widths, chunks=chunks)
    zgs = dp // (NX * NYH * CLS)
    half = tok // 2
    wide = max(widths)
    rows = wide // NX
    br = rows // (CLS * NYH)
    pieces = [w // (2 * dp) for w in widths]
    scratch = [
        pltpu.SMEM((2, 1), F32),
        pltpu.VMEM((tok, wide), BF16),
        pltpu.VMEM((cols, wide), BF16),
        pltpu.VMEM((wide // 2, wide // 2), BF16),
        pltpu.VMEM((wide, tok), BF16),
        pltpu.VMEM((NX, rows, tok), BF16),
        pltpu.VMEM((cols, tok), F32),
        pltpu.VMEM((2, 2, cols, half), BF16),
        pltpu.VMEM((2, tok, cols), BF16),
        pltpu.VMEM((5, 2, cols, half), BF16),
        pltpu.VMEM((2, cols, tok), F32),
        pltpu.VMEM((8, tok), F32),
        pltpu.VMEM((8, tok), F32),
        pltpu.VMEM((8, tok), F32),
        pltpu.VMEM((8, tok), F32),
        pltpu.SemaphoreType.DMA((MSGS,)),
        pltpu.SemaphoreType.DMA((MSGS,)),
        pltpu.SemaphoreType.DMA((4,)),
    ]
    for _, w, z_first in chunks:
        xb = NX if z_first else 1
        xz = br if z_first else 16
        scratch += [
            pltpu.VMEM((w, tok), BF16),
            pltpu.VMEM((w, tok), BF16),
            pltpu.VMEM((1 if z_first else NX, w, tok), BF16),
            pltpu.VMEM((CLS, NYH, xb, br, w), BF16),
            pltpu.VMEM((7, xb, br, w), BF16),
            pltpu.VMEM((NX, xz, w), F32),
            pltpu.VMEM((NX, xz, w), BF16),
            pltpu.VMEM((NX, xz, w), BF16),
            pltpu.VMEM((zgs, 2, 8, w), F32),
            pltpu.VMEM((2, zgs, 8, w), F32),
        ]
    hbm = pl.BlockSpec(memory_space=pltpu.HBM)
    vmem = pl.BlockSpec(memory_space=pltpu.VMEM)
    return pl.pallas_call(
        functools.partial(body, cfg),
        out_shape=tuple(jax.ShapeDtypeStruct((r, cols), F32) for r in pieces),
        in_specs=[hbm] * 6,
        out_specs=(vmem, vmem),
        scratch_shapes=scratch,
        compiler_params=pltpu.CompilerParams(
            collective_id=0, has_side_effects=True, vmem_limit_bytes=61 * 1024 * 1024
        ),
    )(logit_scale, logit_bias, img_feats, txt_feats, w_img.T, w_txt.T)


def column_chunks(cols):
    return ((0, 192, False), (192, 256, True), (448, cols - 448, False))


def stage_order(chunks):
    return (("g", 0), ("g", 1), ("g", 2), ("c", 0), ("1", 1), ("c", 2), ("1", 0), ("x", 1), ("1", 2), ("l", 0), ("l", 1), ("l", 2))


def solution(mesh):
    placed = (P("dp", None), P("dp", None), P(None, "mp"), P(None, "mp"), P(), P())
    return jax.shard_map(
        functools.partial(local, dict(chunks=column_chunks, order=stage_order)),
        mesh=mesh,
        in_specs=placed,
        out_specs=(P(("tower", "dp"), "mp"), P(("tower", "dp"), "mp")),
        check_vma=False,
    )
```

```python
import functools
import math

import jax
import jax.numpy as jnp
from jax import lax
from jax.experimental import pallas as pl
from jax.experimental.pallas import tpu as pltpu
from jax.sharding import PartitionSpec as P

MESH = pl.DeviceIdType.MESH
EPS = 1e-06
NX, NYH, CLS = 4, 2, 4
MSGS = 128
VMEM_BYTES = 53 * 2**20 + 6 * 2**17
F32 = jnp.float32
BF16 = jnp.bfloat16


def dot_nt(a, b):
    return lax.dot_general(a, b, (((1,), (1,)), ((), ())), preferred_element_type=F32)


def dot_nn(a, b):
    return jnp.dot(a, b, preferred_element_type=F32)


def col_to_rows(col):
    n = col.shape[0]
    return jnp.transpose(jnp.broadcast_to(col, (n, 128)))[:8]


def body(cfg, scale_ref, bias_ref, img_ref, txt_ref, wi_ref, wt_ref, out_img, out_txt, *scratch):
    (smem, feats, weights, perm, feats_t, fx, proj, own_t, own_n, win, acc) = scratch[:11]
    (sq_out, sq_in, inner_out, inner_in, inv_mine, inv_win, ssem, rsem, lsem) = scratch[11:20]
    rest = scratch[20:]
    dp, tok, widths, chunks = cfg["dp"], cfg["tok"], cfg["widths"], cfg["chunks"]
    zgs = dp // (NX * NYH * CLS)
    zs = zgs * CLS
    half = tok // 2
    pieces = [w // (2 * dp) for w in widths]
    names = ("ps", "pr", "gx", "cb", "l1", "xf", "xs", "xr", "st", "l2")
    buf = [dict(zip(names, rest[len(names) * q : len(names) * (q + 1)])) for q in range(len(chunks))]

    t, d, m = lax.axis_index("tower"), lax.axis_index("dp"), lax.axis_index("mp")
    x = d // (NYH * zs)
    yh = (d // zs) % NYH
    z = d % zs
    zl, zg = z % CLS, z // CLS
    h = (m + yh) % 2

    def at(xx, yy, zz):
        return (xx * NYH + yy) * zs + zz

    def along_z(dz, dy):
        return (t, at(x, (yh + dy) % NYH, (z + dz + zs) % zs), m)

    def block(k):
        b = (d + k + dp) % dp
        return b, (h + (b // zs) % NYH) % 2

    partner = (t, d, 1 - m)
    cross = {k: (1 - t,) + block(k) for k in (0, 1, -1)}
    onward = {k: (t,) + block(k) for k in (1, -1)}
    x_dev = {j: (t, at((x + j) % NX, yh, z), m) for j in (1, 2, 3)}
    two = {}
    for dy in range(NYH):
        yy = (yh + dy) % NYH
        two[dy] = (t, at(x, yy, (z + 2 - 4 * yy + zs) % zs), m)
    last = {(j, dt): ((t + dt) % 2, at(x, yh, ((zg + j) % zgs) * CLS + zl), m) for j in range(zgs) for dt in range(2)}
    del last[0, 0]

    peers = [cross[0], cross[1], cross[-1], onward[1], onward[-1]]
    peers += [along_z(dz, dy) for dz in (1, -1, 2, -2) for dy in range(NYH)]
    peers += [dev for (j, dt), dev in last.items() if j]
    peers += list(x_dev.values()) + [along_z(0, 1), partner]

    def loads(which):
        f, w, n = (img_ref, txt_ref)[which], (wi_ref, wt_ref)[which], widths[which] // 2
        out = []
        for part in range(2):
            k = pl.ds(part * n, n)
            out.append(pltpu.make_async_copy(f.at[:, k], feats.at[:, k], lsem.at[2 * part]))
            out.append(pltpu.make_async_copy(w.at[:, k], weights.at[:, k], lsem.at[2 * part + 1]))
        out.append(pltpu.make_async_copy(scale_ref, smem.at[0], lsem.at[4]))
        out.append(pltpu.make_async_copy(bias_ref, smem.at[1], lsem.at[5]))
        return out

    def start_loads(which):
        for c in loads(which):
            c.start()

    for which in range(2):
        pl.when(t == which)(functools.partial(start_loads, which))

    barrier = pltpu.get_barrier_semaphore()
    for dev in peers:
        pl.semaphore_signal(barrier, inc=1, device_id=dev, device_id_type=MESH)

    ids = {}
    started = {0: [], 1: [], None: []}

    def copy(key, src, dst, dev):
        n = ids.setdefault(key, len(ids))
        return pltpu.make_async_remote_copy(
            src_ref=src, dst_ref=dst, send_sem=ssem.at[n], recv_sem=rsem.at[n], device_id=dev, device_id_type=MESH
        )

    def send(key, src, dst, dev, which=None, like=None):
        copy(key, src, dst, dev).start()
        started[which].append((key, like or (lambda: dst)))

    def arrive(key, dst):
        copy(key, dst, dst, partner).wait_recv()

    def by_tower(fn, *args):
        for which in range(2):
            pl.when(t == which)(functools.partial(fn, which, *args))

    def project(which):
        n = widths[which] // 2
        ls = loads(which)
        for part in range(2):
            k = slice(part * n, part * n + n)
            ls[2 * part].wait()
            ls[2 * part + 1].wait()
            if part == 0:
                proj[...] = dot_nt(weights[:, k], feats[:, k])
            else:
                proj[...] += dot_nt(weights[:, k], feats[:, k])
        ls[4].wait()
        ls[5].wait()

    def reorder(which):
        wide, r = widths[which], pieces[which]
        n = wide // 2
        row = lax.broadcasted_iota(jnp.int32, (n, 128), 0)
        p = (row * ((65536 + r - 1) // r)) >> 16
        i = row - p * r
        zbits = zgs.bit_length() - 1
        hf, g, y, c, xr = p & 1, (p >> 1) & (zgs - 1), (p >> (1 + zbits)) & 1, (p >> (2 + zbits)) & 3, p >> (4 + zbits)
        col = ((hf * 2 + xr) * NYH + y) * (zs * r) + (g * CLS + c) * r + i
        lane = lax.broadcasted_iota(jnp.int32, (n, 128), 1)
        for c0 in range(0, n, 128):
            cw = min(128, n - c0)
            perm[:n, c0 : c0 + cw] = jnp.where(col == lane + c0, F32(1.0), F32(0.0)).astype(BF16)[:, :cw]
        for xp in range(2):
            a = xp * n // 2
            part = dot_nt(perm[:n, : n // 2], feats[:, a : a + n // 2])
            part = part + dot_nt(perm[:n, n // 2 : n], feats[:, n + a : n + a + n // 2])
            feats_t[xp * n : (xp + 1) * n, :] = part.astype(BF16)
        rows = wide // NX
        for j in (1, 3, 2):
            xs = pl.ds(pl.multiple_of(((x + j) % NX) * rows, 16), rows)
            send(("f", j), feats_t.at[xs], fx.at[x, pl.ds(0, rows)], x_dev[j], which, lambda: fx.at[0, pl.ds(0, rows)])

    by_tower(project)
    value = proj[...]
    squares = jnp.sum(value * value, axis=0, keepdims=True)
    sq_out[...] = jnp.broadcast_to(squares, sq_out.shape)
    value = value.astype(BF16)
    for th in range(2):
        own_t[m, th] = value[:, th * half : (th + 1) * half]
    pl.semaphore_wait(barrier, len(peers))

    cols = cfg["cols"]
    cut = cols // 2
    halves = (pl.ds(0, cut), pl.ds(cut, cols - cut))
    send("sq", sq_out, sq_in, partner)
    for a in range(2):
        send(("e0", a), own_t.at[m, 1 - h, halves[a]], own_t.at[m, 1 - h, halves[a]], partner)
    for s in (1, -1, 0):
        send(("b", s, 0), own_t.at[m, h], win.at[2 - s, m], cross[s])
    send("e1", own_t.at[m, h], own_t.at[m, h], partner)

    arrive("sq", sq_in)
    inv_radius = 1.0 / jnp.sqrt(squares + sq_in[:1] + EPS)
    for th in range(2):
        inv_mine[th] = jnp.broadcast_to(inv_radius[:, th * half : (th + 1) * half], (8, half))
    for s in (1, -1, 0):
        send(("r", s), inv_mine.at[h], inv_win.at[2 - s], cross[s])
    inv_rows = jnp.transpose(jnp.broadcast_to(inv_radius, (half, tok)))

    for a in range(2):
        arrive(("e0", a), own_t.at[1 - m, h, halves[a]])
        for s in (1, -1):
            send(("b", s, 1 + a), own_t.at[1 - m, h, halves[a]], win.at[2 - s, 1 - m, halves[a]], cross[s])
    send(("b", 0, 1), own_t.at[1 - m, h], win.at[2, 1 - m], cross[0])

    def pass_on(s, f):
        side = cross[-s][2]
        c = side if f == 0 else 1 - side
        part = pl.ds(0, cols) if f == 0 else halves[f - 1]
        arrive(("b", s, f), win.at[2 - s, c, part])
        send(("w", s, f), win.at[2 - s, c, part], win.at[2 - 2 * s, c, part], onward[s])

    for s in (1, -1):
        pass_on(s, 0)
    for s in (1, -1):
        arrive(("r", s), inv_win.at[2 - s])
        send(("rw", s), inv_win.at[2 - s], inv_win.at[2 - 2 * s], onward[s])
    arrive("e1", own_t.at[1 - m, 1 - h])
    for f in (1, 2):
        for s in (1, -1):
            pass_on(s, f)
    for c in range(2):
        for th in range(2):
            own_n[c, th * half : (th + 1) * half, :] = jnp.transpose(own_t[c, th])
    by_tower(reorder)

    scale, bias = smem[0, 0], smem[1, 0]
    inv_scale = F32(1.0 / math.sqrt(tok * dp))
    inner = jnp.zeros((tok, half), F32)
    for n, k in enumerate((0, 1, -1, 2, -2)):
        slot = 2 + k
        if k == 0:
            for f in range(2):
                arrive(("b", 0, f), win.at[slot, f])
            arrive(("r", 0), inv_win.at[slot])
        if abs(k) == 2:
            arrive(("rw", -k // 2), inv_win.at[slot])
            arrive(("w", -k // 2, 0), win.at[slot, 0])
            for a in range(2):
                arrive(("w", -k // 2, 1 + a), win.at[slot, 1, halves[a]])
        dots = (dot_nn(own_n[0], win[slot, 0]) + dot_nn(own_n[1], win[slot, 1])) * inv_rows
        inv_cols = inv_win[slot][:1]
        logits = scale * (dots * inv_cols) + bias
        if k == 0:
            rows = lax.broadcasted_iota(jnp.int32, (tok, half), 0)
            columns = lax.broadcasted_iota(jnp.int32, (tok, half), 1) + h * half
            labels = jnp.where(rows == columns, F32(1.0), F32(-1.0))
            coef = -labels * jax.nn.sigmoid(-labels * logits) * inv_scale
        else:
            coef = jax.nn.sigmoid(logits) * inv_scale
        coef = (coef * inv_cols).astype(BF16)
        inner = inner + coef.astype(F32) * dots
        for c in range(2):
            term = dot_nt(win[slot, c], coef)
            if n:
                acc[c] += term
            else:
                acc[c] = term
    inner_out[...] = scale * col_to_rows(jnp.sum(inner, axis=1, keepdims=True))
    send("inner", inner_out, inner_in, partner)
    for q, (c0, w, _) in enumerate(chunks):
        b = buf[q]
        b["ps"][...] = (scale * acc[1 - m, c0 : c0 + w]).astype(BF16)
        send(("p", q), b["ps"], b["pr"], partner)
    arrive("inner", inner_in)
    total_inner = inner_out[:1] + inner_in[:1]

    def stage_g(q):
        c0, w, z_first = chunks[q]
        b = buf[q]
        arrive(("p", q), b["pr"])
        grad = scale * acc[m, c0 : c0 + w] + b["pr"][...].astype(F32)
        grad = (grad - proj[c0 : c0 + w] * (inv_radius * total_inner)) * inv_radius
        own = 0 if z_first else x
        b["gx"][own] = grad.astype(BF16)
        if z_first:
            by_tower(part_products, q)
        else:
            for j in (2, 1, 3):
                send(("x", q, j), b["gx"].at[x], b["gx"].at[x], x_dev[j])

    def send_classes(which, q, br):
        cb, l1 = buf[q]["cb"], buf[q]["l1"]
        rows = pl.ds(0, br)

        def go(slot, c, dy, dev):
            send(("l1", q, slot), cb.at[c % CLS, (yh + dy) % NYH, :, rows], l1.at[slot, :, rows], dev, which, lambda: l1.at[0, :, pl.ds(0, br)])

        for dy in (1, 0):
            go(4 + dy, zl + 2, dy, two[dy])
        for dy in (1, 0):
            go(0 + dy, zl + 1, dy, along_z(1, dy))
            go(2 + dy, zl + 3, dy, along_z(-1, dy))
        go(6, zl, 1, along_z(0, 1))

    def part_products(which, q):
        b = buf[q]
        rows = widths[which] // NX
        br = rows // (CLS * NYH)
        for xx in range(NX):
            total = dot_nt(feats_t[xx * rows : (xx + 1) * rows], b["gx"][0]).astype(BF16)
            for c in range(CLS):
                for y in range(NYH):
                    o = (c * NYH + y) * br
                    b["cb"][c, y, xx, :br] = total[o : o + br]
        send_classes(which, q, br)

    def x_products(which, q):
        b = buf[q]
        gx = b["gx"]
        rows = widths[which] // NX
        br = rows // (CLS * NYH)
        mine = pl.ds(pl.multiple_of(x * rows, 16), rows)
        total = dot_nt(feats_t[mine], gx[x])
        for j in (1, 3, 2):
            src = (x + NX - j) % NX
            if q == first_x:
                arrive(("f", j), fx.at[src, pl.ds(0, rows)])
            arrive(("x", q, j), gx.at[src])
            total += dot_nt(fx[src, :rows], gx[src])
        total = total.astype(BF16)
        for c in range(CLS):
            for y in range(NYH):
                o = (c * NYH + y) * br
                b["cb"][c, y, 0, :br] = total[o : o + br]
        send_classes(which, q, br)

    def class_sum(which, q):
        b = buf[q]
        z_first = chunks[q][2]
        r = pieces[which]
        br = widths[which] // (NX * CLS * NYH)
        for slot in range(7):
            arrive(("l1", q, slot), b["l1"].at[slot, :, pl.ds(0, br)])

        def total(xx):
            s = b["cb"][zl, yh, xx, :br].astype(F32)
            for slot in range(7):
                s = s + b["l1"][slot, xx, :br].astype(F32)
            return s

        if z_first:
            for xx in range(NX):
                s = total(xx)
                b["xf"][xx, :br] = s
                b["xs"][xx, :br] = s.astype(BF16)
            for j in (2, 1, 3):
                src = b["xs"].at[(x + j) % NX, pl.ds(0, br)]
                like = lambda: b["xr"].at[0, pl.ds(0, br)]
                send(("xr", q, j), src, b["xr"].at[j, pl.ds(0, br)], x_dev[j], which, like)
        else:
            send_last(which, q, total(0))

    def x_sum(which, q):
        b = buf[q]
        br = widths[which] // (NX * CLS * NYH)
        s = b["xf"][x, :br]
        for j in (1, 3, 2):
            arrive(("xr", q, j), b["xr"].at[j, pl.ds(0, br)])
            s = s + b["xr"][j, :br].astype(F32)
        send_last(which, q, s)

    def send_last(which, q, s):
        st, l2 = buf[q]["st"], buf[q]["l2"]
        r = pieces[which]
        for g in range(zgs):
            for hf in range(2):
                o = (g * 2 + hf) * r
                st[g, hf, :r] = s[o : o + r]
        l2[t, 0] = st[zg, t]
        for (j, dt), dev in last.items():
            send(("l2", q, j, dt), st.at[(zg + j) % zgs, (t + dt) % 2], l2.at[t, j], dev, which, lambda: l2.at[0, 0])

    def finish(q):
        c0, w, _ = chunks[q]
        l2 = buf[q]["l2"]
        for j, dt in last:
            arrive(("l2", q, j, dt), l2.at[(t + dt) % 2, j])
        a, b = l2[0, 0], l2[1, 0]
        for j in range(1, zgs):
            a, b = a + l2[0, j], b + l2[1, j]
        out_img[:, c0 : c0 + w] = a[: pieces[0]]
        out_txt[:, c0 : c0 + w] = b[: pieces[1]]

    first_x = min(q for q, c in enumerate(chunks) if not c[2])
    for stage, q in cfg["order"](chunks):
        if stage == "g":
            stage_g(q)
        elif stage == "c":
            by_tower(x_products, q)
        elif stage == "1":
            by_tower(class_sum, q)
        elif stage == "x":
            by_tower(x_sum, q)
        else:
            finish(q)

    def drain(which):
        for key, like in started[which]:
            copy(key, like(), like(), partner).wait_send()

    by_tower(drain)
    drain(None)


def local(cfg, img_feats, txt_feats, w_img, w_txt, logit_scale, logit_bias):
    dp = lax.axis_size("dp")
    tok = img_feats.shape[0]
    widths = (img_feats.shape[1], txt_feats.shape[1])
    cols = w_img.shape[1]
    chunks = cfg["chunks"](cols)
    cfg = dict(cfg, cols=cols, dp=dp, tok=tok, widths=widths, chunks=chunks)
    zgs = dp // (NX * NYH * CLS)
    half = tok // 2
    wide = max(widths)
    rows = wide // NX
    br = rows // (CLS * NYH)
    pieces = [w // (2 * dp) for w in widths]
    scratch = [
        pltpu.SMEM((2, 1), F32),
        pltpu.VMEM((tok, wide), BF16),
        pltpu.VMEM((cols, wide), BF16),
        pltpu.VMEM((wide // 2, wide // 2), BF16),
        pltpu.VMEM((wide, tok), BF16),
        pltpu.VMEM((NX, rows, tok), BF16),
        pltpu.VMEM((cols, tok), F32),
        pltpu.VMEM((2, 2, cols, half), BF16),
        pltpu.VMEM((2, tok, cols), BF16),
        pltpu.VMEM((5, 2, cols, half), BF16),
        pltpu.VMEM((2, cols, tok), F32),
        pltpu.VMEM((8, tok), F32),
        pltpu.VMEM((8, tok), F32),
        pltpu.VMEM((8, tok), F32),
        pltpu.VMEM((8, tok), F32),
        pltpu.VMEM((2, 8, half), F32),
        pltpu.VMEM((5, 8, half), F32),
        pltpu.SemaphoreType.DMA((MSGS,)),
        pltpu.SemaphoreType.DMA((MSGS,)),
        pltpu.SemaphoreType.DMA((6,)),
    ]
    for _, w, z_first in chunks:
        xb = NX if z_first else 1
        xz = br if z_first else 16
        scratch += [
            pltpu.VMEM((w, tok), BF16),
            pltpu.VMEM((w, tok), BF16),
            pltpu.VMEM((1 if z_first else NX, w, tok), BF16),
            pltpu.VMEM((CLS, NYH, xb, br, w), BF16),
            pltpu.VMEM((7, xb, br, w), BF16),
            pltpu.VMEM((NX, xz, w), F32),
            pltpu.VMEM((NX, xz, w), BF16),
            pltpu.VMEM((NX, xz, w), BF16),
            pltpu.VMEM((zgs, 2, 8, w), F32),
            pltpu.VMEM((2, zgs, 8, w), F32),
        ]
    hbm = pl.BlockSpec(memory_space=pltpu.HBM)
    vmem = pl.BlockSpec(memory_space=pltpu.VMEM)
    return pl.pallas_call(
        functools.partial(body, cfg),
        out_shape=tuple(jax.ShapeDtypeStruct((r, cols), F32) for r in pieces),
        in_specs=[hbm] * 6,
        out_specs=(vmem, vmem),
        scratch_shapes=scratch,
        compiler_params=pltpu.CompilerParams(
            collective_id=0, has_side_effects=True, vmem_limit_bytes=VMEM_BYTES
        ),
    )(logit_scale, logit_bias, img_feats, txt_feats, w_img.T, w_txt.T)


def column_chunks(cols):
    return ((0, 256, False), (256, 128, True), (384, cols - 384, False))


def stage_order(chunks):
    return (("g", 0), ("g", 1), ("g", 2), ("c", 0), ("1", 1), ("c", 2), ("1", 0), ("x", 1), ("1", 2), ("l", 0), ("l", 1), ("l", 2))


def solution(mesh):
    placed = (P("dp", None), P("dp", None), P(None, "mp"), P(None, "mp"), P(), P())
    return jax.shard_map(
        functools.partial(local, dict(chunks=column_chunks, order=stage_order)),
        mesh=mesh,
        in_specs=placed,
        out_specs=(P(("tower", "dp"), "mp"), P(("tower", "dp"), "mp")),
        check_vma=False,
    )
```

```python
import functools
import math

import jax
import jax.numpy as jnp
from jax import lax
from jax.experimental import pallas as pl
from jax.experimental.pallas import tpu as pltpu
from jax.sharding import PartitionSpec as P

MESH = pl.DeviceIdType.MESH
EPS = 1e-06
NX, NYH, CLS = 4, 2, 4
MSGS = 128
ORDER = ("g0", "g1", "g2", "g3", "c0", "11", "c2", "10", "c3", "x1", "12", "13", "l0", "l1", "l2", "l3")
VMEM_BYTES = 53 * 2**20 + 6 * 2**17
F32 = jnp.float32
BF16 = jnp.bfloat16


def dot_nt(a, b):
    return lax.dot_general(a, b, (((1,), (1,)), ((), ())), preferred_element_type=F32)


def dot_nn(a, b):
    return jnp.dot(a, b, preferred_element_type=F32)


def col_to_rows(col):
    n = col.shape[0]
    return jnp.transpose(jnp.broadcast_to(col, (n, 128)))[:8]


def body(cfg, scale_ref, bias_ref, img_ref, txt_ref, wi_ref, wt_ref, out_img, out_txt, *scratch):
    (smem, feats, weights, perm, feats_t, fx, proj, own_t, own_n, win, acc) = scratch[:11]
    (sq_out, sq_in, inner_out, inner_in, inv_mine, inv_win, ssem, rsem, lsem) = scratch[11:20]
    rest = scratch[20:]
    dp, tok, widths, chunks = cfg["dp"], cfg["tok"], cfg["widths"], cfg["chunks"]
    zgs = dp // (NX * NYH * CLS)
    zs = zgs * CLS
    half = tok // 2
    pieces = [w // (2 * dp) for w in widths]
    names = ("ps", "pr", "gx", "cb", "l1", "xf", "xs", "xr", "st", "l2")
    buf = [dict(zip(names, rest[len(names) * q : len(names) * (q + 1)])) for q in range(len(chunks))]

    t, d, m = lax.axis_index("tower"), lax.axis_index("dp"), lax.axis_index("mp")
    x = d // (NYH * zs)
    yh = (d // zs) % NYH
    z = d % zs
    zl, zg = z % CLS, z // CLS
    h = (m + yh) % 2

    def at(xx, yy, zz):
        return (xx * NYH + yy) * zs + zz

    def along_z(dz, dy):
        return (t, at(x, (yh + dy) % NYH, (z + dz + zs) % zs), m)

    def block(k):
        b = (d + k + dp) % dp
        return b, (h + (b // zs) % NYH) % 2

    partner = (t, d, 1 - m)
    cross = {k: (1 - t,) + block(k) for k in (0, 1, -1)}
    onward = {k: (t,) + block(k) for k in (1, -1)}
    x_dev = {j: (t, at((x + j) % NX, yh, z), m) for j in (1, 2, 3)}
    two = {}
    for dy in range(NYH):
        yy = (yh + dy) % NYH
        two[dy] = (t, at(x, yy, (z + 2 - 4 * yy + zs) % zs), m)
    last = {(j, dt): ((t + dt) % 2, at(x, yh, ((zg + j) % zgs) * CLS + zl), m) for j in range(zgs) for dt in range(2)}
    del last[0, 0]

    peers = [cross[0], cross[1], cross[-1], onward[1], onward[-1]]
    peers += [along_z(dz, dy) for dz in (1, -1, 2, -2) for dy in range(NYH)]
    peers += [dev for (j, dt), dev in last.items() if j]
    peers += list(x_dev.values()) + [along_z(0, 1), partner]

    def loads(which):
        f, w, n = (img_ref, txt_ref)[which], (wi_ref, wt_ref)[which], widths[which] // 2
        out = []
        for part in range(2):
            k = pl.ds(part * n, n)
            out.append(pltpu.make_async_copy(f.at[:, k], feats.at[:, k], lsem.at[2 * part]))
            out.append(pltpu.make_async_copy(w.at[:, k], weights.at[:, k], lsem.at[2 * part + 1]))
        out.append(pltpu.make_async_copy(scale_ref, smem.at[0], lsem.at[4]))
        out.append(pltpu.make_async_copy(bias_ref, smem.at[1], lsem.at[5]))
        return out

    def start_loads(which):
        for c in loads(which):
            c.start()

    for which in range(2):
        pl.when(t == which)(functools.partial(start_loads, which))

    barrier = pltpu.get_barrier_semaphore()
    for dev in peers:
        pl.semaphore_signal(barrier, inc=1, device_id=dev, device_id_type=MESH)

    ids = {}
    started = {0: [], 1: [], None: []}

    def copy(key, src, dst, dev):
        n = ids.setdefault(key, len(ids))
        return pltpu.make_async_remote_copy(
            src_ref=src, dst_ref=dst, send_sem=ssem.at[n], recv_sem=rsem.at[n], device_id=dev, device_id_type=MESH
        )

    def send(key, src, dst, dev, which=None, like=None):
        copy(key, src, dst, dev).start()
        started[which].append((key, like or (lambda: dst)))

    def arrive(key, dst):
        copy(key, dst, dst, partner).wait_recv()

    def by_tower(fn, *args):
        for which in range(2):
            pl.when(t == which)(functools.partial(fn, which, *args))

    def project(which):
        n = widths[which] // 2
        ls = loads(which)
        for part in range(2):
            k = slice(part * n, part * n + n)
            ls[2 * part].wait()
            ls[2 * part + 1].wait()
            if part == 0:
                proj[...] = dot_nt(weights[:, k], feats[:, k])
            else:
                proj[...] += dot_nt(weights[:, k], feats[:, k])
        ls[4].wait()
        ls[5].wait()

    def reorder(which):
        wide, r = widths[which], pieces[which]
        n = wide // 2
        row = lax.broadcasted_iota(jnp.int32, (n, 128), 0)
        p = (row * ((65536 + r - 1) // r)) >> 16
        i = row - p * r
        zbits = zgs.bit_length() - 1
        hf, g, y, c, xr = p & 1, (p >> 1) & (zgs - 1), (p >> (1 + zbits)) & 1, (p >> (2 + zbits)) & 3, p >> (4 + zbits)
        col = ((hf * 2 + xr) * NYH + y) * (zs * r) + (g * CLS + c) * r + i
        lane = lax.broadcasted_iota(jnp.int32, (n, 128), 1)
        for c0 in range(0, n, 128):
            cw = min(128, n - c0)
            perm[:n, c0 : c0 + cw] = jnp.where(col == lane + c0, F32(1.0), F32(0.0)).astype(BF16)[:, :cw]
        for xp in range(2):
            a = xp * n // 2
            part = dot_nt(perm[:n, : n // 2], feats[:, a : a + n // 2])
            part = part + dot_nt(perm[:n, n // 2 : n], feats[:, n + a : n + a + n // 2])
            feats_t[xp * n : (xp + 1) * n, :] = part.astype(BF16)
        rows = wide // NX
        for j in (1, 3, 2):
            xs = pl.ds(pl.multiple_of(((x + j) % NX) * rows, 16), rows)
            send(("f", j), feats_t.at[xs], fx.at[x, pl.ds(0, rows)], x_dev[j], which, lambda: fx.at[0, pl.ds(0, rows)])

    by_tower(project)
    value = proj[...]
    squares = jnp.sum(value * value, axis=0, keepdims=True)
    sq_out[...] = jnp.broadcast_to(squares, sq_out.shape)
    value = value.astype(BF16)
    for th in range(2):
        own_t[m, th] = value[:, th * half : (th + 1) * half]
    pl.semaphore_wait(barrier, len(peers))

    cols = cfg["cols"]
    cut = cols // 2
    halves = (pl.ds(0, cut), pl.ds(cut, cols - cut))
    send("sq", sq_out, sq_in, partner)
    for a in range(2):
        send(("e0", a), own_t.at[m, 1 - h, halves[a]], own_t.at[m, 1 - h, halves[a]], partner)
    for s in (1, -1, 0):
        send(("b", s, 0), own_t.at[m, h], win.at[2 - s, m], cross[s])
    send("e1", own_t.at[m, h], own_t.at[m, h], partner)

    arrive("sq", sq_in)
    inv_radius = 1.0 / jnp.sqrt(squares + sq_in[:1] + EPS)
    for th in range(2):
        inv_mine[th] = jnp.broadcast_to(inv_radius[:, th * half : (th + 1) * half], (8, half))
    for s in (1, -1, 0):
        send(("r", s), inv_mine.at[h], inv_win.at[2 - s], cross[s])
    inv_rows = jnp.transpose(jnp.broadcast_to(inv_radius, (half, tok)))

    for a in range(2):
        arrive(("e0", a), own_t.at[1 - m, h, halves[a]])
        for s in (1, -1):
            send(("b", s, 1 + a), own_t.at[1 - m, h, halves[a]], win.at[2 - s, 1 - m, halves[a]], cross[s])
    send(("b", 0, 1), own_t.at[1 - m, h], win.at[2, 1 - m], cross[0])

    def pass_on(s, f):
        side = cross[-s][2]
        c = side if f == 0 else 1 - side
        part = pl.ds(0, cols) if f == 0 else halves[f - 1]
        arrive(("b", s, f), win.at[2 - s, c, part])
        send(("w", s, f), win.at[2 - s, c, part], win.at[2 - 2 * s, c, part], onward[s])

    for s in (1, -1):
        pass_on(s, 0)
    for s in (1, -1):
        arrive(("r", s), inv_win.at[2 - s])
        send(("rw", s), inv_win.at[2 - s], inv_win.at[2 - 2 * s], onward[s])
    arrive("e1", own_t.at[1 - m, 1 - h])
    for f in (1, 2):
        for s in (1, -1):
            pass_on(s, f)
    for c in range(2):
        for th in range(2):
            own_n[c, th * half : (th + 1) * half, :] = jnp.transpose(own_t[c, th])
    scale, bias = smem[0, 0], smem[1, 0]
    inv_scale = F32(1.0 / math.sqrt(tok * dp))
    inner = jnp.zeros((tok, half), F32)
    for n, k in enumerate((0, 1, -1, 2, -2)):
        slot = 2 + k
        if k == 0:
            for f in range(2):
                arrive(("b", 0, f), win.at[slot, f])
            arrive(("r", 0), inv_win.at[slot])
        if n == 3:
            by_tower(reorder)
        if abs(k) == 2:
            arrive(("rw", -k // 2), inv_win.at[slot])
            arrive(("w", -k // 2, 0), win.at[slot, 0])
            for a in range(2):
                arrive(("w", -k // 2, 1 + a), win.at[slot, 1, halves[a]])
        dots = (dot_nn(own_n[0], win[slot, 0]) + dot_nn(own_n[1], win[slot, 1])) * inv_rows
        inv_cols = inv_win[slot][:1]
        logits = scale * (dots * inv_cols) + bias
        if k == 0:
            rows = lax.broadcasted_iota(jnp.int32, (tok, half), 0)
            columns = lax.broadcasted_iota(jnp.int32, (tok, half), 1) + h * half
            labels = jnp.where(rows == columns, F32(1.0), F32(-1.0))
            coef = -labels * jax.nn.sigmoid(-labels * logits) * inv_scale
        else:
            coef = jax.nn.sigmoid(logits) * inv_scale
        coef = (coef * inv_cols).astype(BF16)
        inner = inner + coef.astype(F32) * dots
        for c in range(2):
            term = dot_nt(win[slot, c], coef)
            if n:
                acc[c] += term
            else:
                acc[c] = term
    inner_out[...] = scale * col_to_rows(jnp.sum(inner, axis=1, keepdims=True))
    send("inner", inner_out, inner_in, partner)
    for q, (c0, w, _) in enumerate(chunks):
        b = buf[q]
        b["ps"][...] = (scale * acc[1 - m, c0 : c0 + w]).astype(BF16)
        send(("p", q), b["ps"], b["pr"], partner)
    arrive("inner", inner_in)
    total_inner = inner_out[:1] + inner_in[:1]

    def stage_g(q):
        c0, w, z_first = chunks[q]
        b = buf[q]
        arrive(("p", q), b["pr"])
        grad = scale * acc[m, c0 : c0 + w] + b["pr"][...].astype(F32)
        grad = (grad - proj[c0 : c0 + w] * (inv_radius * total_inner)) * inv_radius
        own = 0 if z_first else x
        b["gx"][own] = grad.astype(BF16)
        if z_first:
            by_tower(part_products, q)
        else:
            for j in (2, 1, 3):
                send(("x", q, j), b["gx"].at[x], b["gx"].at[x], x_dev[j])

    def send_classes(which, q, br):
        cb, l1 = buf[q]["cb"], buf[q]["l1"]
        rows = pl.ds(0, br)

        def go(slot, c, dy, dev):
            send(("l1", q, slot), cb.at[c % CLS, (yh + dy) % NYH, :, rows], l1.at[slot, :, rows], dev, which, lambda: l1.at[0, :, pl.ds(0, br)])

        for dy in (1, 0):
            go(4 + dy, zl + 2, dy, two[dy])
        for dy in (1, 0):
            go(0 + dy, zl + 1, dy, along_z(1, dy))
            go(2 + dy, zl + 3, dy, along_z(-1, dy))
        go(6, zl, 1, along_z(0, 1))

    def part_products(which, q):
        b = buf[q]
        rows = widths[which] // NX
        br = rows // (CLS * NYH)
        for xx in range(NX):
            total = dot_nt(feats_t[xx * rows : (xx + 1) * rows], b["gx"][0]).astype(BF16)
            for c in range(CLS):
                for y in range(NYH):
                    o = (c * NYH + y) * br
                    b["cb"][c, y, xx, :br] = total[o : o + br]
        send_classes(which, q, br)

    def x_products(which, q):
        b = buf[q]
        gx = b["gx"]
        rows = widths[which] // NX
        br = rows // (CLS * NYH)
        mine = pl.ds(pl.multiple_of(x * rows, 16), rows)
        total = dot_nt(feats_t[mine], gx[x])
        for j in (1, 3, 2):
            src = (x + NX - j) % NX
            if q == first_x:
                arrive(("f", j), fx.at[src, pl.ds(0, rows)])
            arrive(("x", q, j), gx.at[src])
            total += dot_nt(fx[src, :rows], gx[src])
        total = total.astype(BF16)
        for c in range(CLS):
            for y in range(NYH):
                o = (c * NYH + y) * br
                b["cb"][c, y, 0, :br] = total[o : o + br]
        send_classes(which, q, br)

    def class_sum(which, q):
        b = buf[q]
        z_first = chunks[q][2]
        r = pieces[which]
        br = widths[which] // (NX * CLS * NYH)
        for slot in range(7):
            arrive(("l1", q, slot), b["l1"].at[slot, :, pl.ds(0, br)])

        def total(xx):
            s = b["cb"][zl, yh, xx, :br].astype(F32)
            for slot in range(7):
                s = s + b["l1"][slot, xx, :br].astype(F32)
            return s

        if z_first:
            for xx in range(NX):
                s = total(xx)
                b["xf"][xx, :br] = s
                b["xs"][xx, :br] = s.astype(BF16)
            for j in (2, 1, 3):
                src = b["xs"].at[(x + j) % NX, pl.ds(0, br)]
                like = lambda: b["xr"].at[0, pl.ds(0, br)]
                send(("xr", q, j), src, b["xr"].at[j, pl.ds(0, br)], x_dev[j], which, like)
        else:
            send_last(which, q, total(0))

    def x_sum(which, q):
        b = buf[q]
        br = widths[which] // (NX * CLS * NYH)
        s = b["xf"][x, :br]
        for j in (1, 3, 2):
            arrive(("xr", q, j), b["xr"].at[j, pl.ds(0, br)])
            s = s + b["xr"][j, :br].astype(F32)
        send_last(which, q, s)

    def send_last(which, q, s):
        st, l2 = buf[q]["st"], buf[q]["l2"]
        r = pieces[which]
        for g in range(zgs):
            for hf in range(2):
                o = (g * 2 + hf) * r
                st[g, hf, :r] = s[o : o + r]
        l2[t, 0] = st[zg, t]
        for (j, dt), dev in last.items():
            send(("l2", q, j, dt), st.at[(zg + j) % zgs, (t + dt) % 2], l2.at[t, j], dev, which, lambda: l2.at[0, 0])

    def finish(q):
        c0, w, _ = chunks[q]
        l2 = buf[q]["l2"]
        for j, dt in last:
            arrive(("l2", q, j, dt), l2.at[(t + dt) % 2, j])
        a, b = l2[0, 0], l2[1, 0]
        for j in range(1, zgs):
            a, b = a + l2[0, j], b + l2[1, j]
        out_img[:, c0 : c0 + w] = a[: pieces[0]]
        out_txt[:, c0 : c0 + w] = b[: pieces[1]]

    first_x = min(q for q, c in enumerate(chunks) if not c[2])
    for stage, q in cfg["order"](chunks):
        if stage == "g":
            stage_g(q)
        elif stage == "c":
            by_tower(x_products, q)
        elif stage == "1":
            by_tower(class_sum, q)
        elif stage == "x":
            by_tower(x_sum, q)
        else:
            finish(q)

    def drain(which):
        for key, like in started[which]:
            copy(key, like(), like(), partner).wait_send()

    by_tower(drain)
    drain(None)


def local(cfg, img_feats, txt_feats, w_img, w_txt, logit_scale, logit_bias):
    dp = lax.axis_size("dp")
    tok = img_feats.shape[0]
    widths = (img_feats.shape[1], txt_feats.shape[1])
    cols = w_img.shape[1]
    chunks = cfg["chunks"](cols)
    cfg = dict(cfg, cols=cols, dp=dp, tok=tok, widths=widths, chunks=chunks)
    zgs = dp // (NX * NYH * CLS)
    half = tok // 2
    wide = max(widths)
    rows = wide // NX
    br = rows // (CLS * NYH)
    pieces = [w // (2 * dp) for w in widths]
    scratch = [
        pltpu.SMEM((2, 1), F32),
        pltpu.VMEM((tok, wide), BF16),
        pltpu.VMEM((cols, wide), BF16),
        pltpu.VMEM((wide // 2, wide // 2), BF16),
        pltpu.VMEM((wide, tok), BF16),
        pltpu.VMEM((NX, rows, tok), BF16),
        pltpu.VMEM((cols, tok), F32),
        pltpu.VMEM((2, 2, cols, half), BF16),
        pltpu.VMEM((2, tok, cols), BF16),
        pltpu.VMEM((5, 2, cols, half), BF16),
        pltpu.VMEM((2, cols, tok), F32),
        pltpu.VMEM((8, tok), F32),
        pltpu.VMEM((8, tok), F32),
        pltpu.VMEM((8, tok), F32),
        pltpu.VMEM((8, tok), F32),
        pltpu.VMEM((2, 8, half), F32),
        pltpu.VMEM((5, 8, half), F32),
        pltpu.SemaphoreType.DMA((MSGS,)),
        pltpu.SemaphoreType.DMA((MSGS,)),
        pltpu.SemaphoreType.DMA((6,)),
    ]
    for _, w, z_first in chunks:
        xb = NX if z_first else 1
        xz = br if z_first else 16
        scratch += [
            pltpu.VMEM((w, tok), BF16),
            pltpu.VMEM((w, tok), BF16),
            pltpu.VMEM((1 if z_first else NX, w, tok), BF16),
            pltpu.VMEM((CLS, NYH, xb, br, w), BF16),
            pltpu.VMEM((7, xb, br, w), BF16),
            pltpu.VMEM((NX, xz, w), F32),
            pltpu.VMEM((NX, xz, w), BF16),
            pltpu.VMEM((NX, xz, w), BF16),
            pltpu.VMEM((zgs, 2, 8, w), F32),
            pltpu.VMEM((2, zgs, 8, w), F32),
        ]
    hbm = pl.BlockSpec(memory_space=pltpu.HBM)
    vmem = pl.BlockSpec(memory_space=pltpu.VMEM)
    return pl.pallas_call(
        functools.partial(body, cfg),
        out_shape=tuple(jax.ShapeDtypeStruct((r, cols), F32) for r in pieces),
        in_specs=[hbm] * 6,
        out_specs=(vmem, vmem),
        scratch_shapes=scratch,
        compiler_params=pltpu.CompilerParams(
            collective_id=0, has_side_effects=True, vmem_limit_bytes=VMEM_BYTES
        ),
    )(logit_scale, logit_bias, img_feats, txt_feats, w_img.T, w_txt.T)


def column_chunks(cols):
    return ((0, 128, False), (128, 128, True), (256, 128, False), (384, cols - 384, False))


def stage_order(chunks):
    return tuple((s[0], int(s[1])) for s in ORDER)


def solution(mesh):
    placed = (P("dp", None), P("dp", None), P(None, "mp"), P(None, "mp"), P(), P())
    return jax.shard_map(
        functools.partial(local, dict(chunks=column_chunks, order=stage_order)),
        mesh=mesh,
        in_specs=placed,
        out_specs=(P(("tower", "dp"), "mp"), P(("tower", "dp"), "mp")),
        check_vma=False,
    )
```
